512 devices in a mesh: frame: 16 (over z_hi, y), pix: 32 (over z_lo, x, core).
Axes of the slice: x: 4, y: 4, z: 16 (z_hi: 4, z_lo: 4; z = z_hi * 4 + z_lo), core: 2. Of those that a mesh axis runs over, the one named last changes fastest.
Arguments:
- intensity: bfloat16 [512, 262144], P('frame', 'pix'), may hold values from 0.099609375 to 10
- labels: int32 [262144], P('pix'), may hold values from -1 to 63, as said below
Outputs:
- two_time: float32 [64, 512, 512], P('pix', 'frame')
The draws below stay inside these ranges and needn't reach their ends.
Inputs may be any that keep to these rules, and one draw needn't show every extreme that they name: `labels`: on the pixels of one index of pix every q-bin label occurs at least 64 and at most 128 times and -1 occurs; one label occurs exactly 128 times on every index of pix.
All inputs are finite; a program needn't handle non-finite values.
Results may differ from the reference program's by a relative error of at most 0.0003.
Values may be sent and summed in bfloat16 or wider, within the bound.
A program may use at most 64 MiB of HBM per device.

```python
import math
import jax
import jax.numpy as jnp
from jax import lax

BINS = 64
FRAMES = 512
PIX_DEV = 8192
PIXELS = 262144
N_PIX = 32


def draw_labels(key, part):
    key = jax.random.fold_in(key, 7)
    shards = PIXELS // PIX_DEV
    most = PIX_DEV // BINS
    full_key, low_key, count_key, perm_key = jax.random.split(key, 4)
    full_bin = jax.random.randint(full_key, (), 0, BINS)
    low_bin = (full_bin + 1 + jax.random.randint(low_key, (shards,), 0, BINS - 1)) % BINS
    bin_counts = jax.random.randint(count_key, (shards, BINS), most // 2, most + 1)
    bin_ids = jnp.arange(BINS, dtype=jnp.int32)
    bin_counts = jnp.where(bin_ids[None, :] == full_bin, most, bin_counts)
    bin_counts = jnp.where(bin_ids[None, :] == low_bin[:, None], most // 2, bin_counts)
    bin_ends = jnp.cumsum(bin_counts, axis=1)
    slots = jnp.arange(PIX_DEV, dtype=jnp.int32)
    label_rows = jnp.sum((slots[None, :, None] >= bin_ends[:, None, :]).astype(jnp.int32), axis=2)
    label_rows = jnp.where(label_rows >= BINS, -1, label_rows)
    row_keys = jax.random.split(perm_key, shards)
    label_rows = jax.vmap(lambda row_key, row: jax.random.permutation(row_key, row))(row_keys, label_rows)
    return label_rows.reshape(PIXELS).astype(jnp.int32)


def levels(rng, dims, pieces, least, high):
    def one(position, parts):
        heights = jax.random.uniform(jax.random.fold_in(jax.random.fold_in(rng, 6), position), (parts,), jnp.float32, least / len(pieces), high / len(pieces))
        return jnp.repeat(jnp.exp(heights), dims[position] // parts).reshape((-1,) + (1,) * (len(dims) - position - 1))

    loudness = one(*pieces[0])
    for cut in pieces[1:]:
        loudness = loudness * one(*cut)
    return loudness


def setup_inputs(seed: int = 0) -> dict:
    key_list = jax.random.split(jax.random.key(seed), 3)
    intensity = jnp.clip(jnp.exp(math.log(10.0) - 4.609084 * jax.random.uniform(key_list[0], (FRAMES, PIXELS), jnp.float32) ** levels(key_list[0], (FRAMES, PIXELS), ((0, 16), (1, 32)), -0.2, 0.2)), 0.099609375, 10.0).astype(jnp.bfloat16)
    labels = draw_labels(jax.random.fold_in(key_list[2], 71), 0)
    return dict(intensity=intensity, labels=labels)


def reference(intensity, labels):
    pix_order = jnp.argsort(labels, stable=True).astype(jnp.int32)
    sorted_labels = labels[pix_order]
    bin_ids = jnp.arange(BINS, dtype=jnp.int32)
    starts = jnp.searchsorted(sorted_labels, bin_ids, side="left").astype(jnp.int32)
    bin_ends = jnp.searchsorted(sorted_labels, bin_ids, side="right").astype(jnp.int32)
    window = N_PIX * (PIX_DEV // BINS)
    columns = jnp.concatenate([intensity[:, pix_order], jnp.zeros((FRAMES, window), intensity.dtype)], axis=1)
    offsets = jnp.arange(window, dtype=jnp.int32)

    def one_bin(which):
        first_col = starts[which]
        bin_count = bin_ends[which] - first_col
        block = lax.dynamic_slice_in_dim(columns, first_col, window, 1).astype(jnp.float32)
        keep_mask = (offsets < bin_count).astype(jnp.float32)
        block = block * keep_mask[None, :]
        gram_bin = jnp.dot(block, block.T, precision=lax.Precision.HIGHEST)
        return gram_bin, jnp.sum(block, axis=1), bin_count.astype(jnp.float32)

    gram, totals, counts = lax.map(one_bin, bin_ids)
    return counts[:, None, None] * gram / (totals[:, :, None] * totals[:, None, :])
```

```python
import jax
import jax.numpy as jnp
from jax import lax
from jax.experimental import pallas as pl
from jax.experimental.pallas import tpu as pltpu
from jax.sharding import PartitionSpec as P

MESH = pl.DeviceIdType.MESH
BF16, F32, I32 = jnp.bfloat16, jnp.float32, jnp.int32
MSG = 296


def iota(shape, dim):
    return lax.broadcasted_iota(I32, shape, dim)


def slot_sources(lab, onehot, weighted, ranked, cum, idx):
    bins = iota((64, 128), 0)
    lane = iota((64, 128), 1).astype(F32)
    for i in range(64):
        member = (lab[i : i + 1, :] == bins).astype(F32)
        onehot[pl.ds(i * 64, 64), :] = member.astype(BF16)
        weighted[0:64, pl.ds(i * 128, 128)] = (member * (i + 1.0)).astype(BF16)
        weighted[64:128, pl.ds(i * 128, 128)] = (member * lane).astype(BF16)
    row, col = iota((128, 256), 0), iota((128, 256), 1)
    upto = ((row <= col) | (col >= 128)).astype(F32).astype(BF16)
    cum[...] = jnp.dot(onehot[...], upto, preferred_element_type=F32)
    before = jnp.zeros((64, 128), F32)
    slot = iota((128, 128), 0).astype(F32)
    for i in range(64):
        member = onehot[pl.ds(i * 64, 64), :].astype(F32)
        through = cum[pl.ds(i * 64, 64), 0:128] + before
        rank = jnp.sum(member * through, axis=0, keepdims=True) - 1.0
        before = before + cum[pl.ds(i * 64, 64), 128:256]
        ranked[:, pl.ds(i * 128, 128)] = (slot == rank).astype(F32).astype(BF16)
    found = lax.dot_general(
        weighted[...], ranked[...], (((1,), (1,)), ((), ())), preferred_element_type=F32
    )
    idx[...] = found.astype(I32)


def kernel(
    lab_hbm, x_hbm, o_ref,
    lab, xin, onehot, weighted, ranked, cum, idx, src, packed, met, part, got, half, xgot, tcol, fin, out,
    load_sem, send_sem, met_sem, core_send, core_recv, x_send, x_recv, fin_send, fin_recv,
):
    f, p = lax.axis_index("frame"), lax.axis_index("pix")
    zh, y = f // 4, f % 4
    zl, x, c = p // 8, (p // 2) % 4, p % 2
    z = zh * 4 + zl
    own_bin = zl * 16 + f
    owner_p = own_bin // 2
    to_self = jnp.logical_and(owner_p == p, f % 2 == c)

    load_lab = pltpu.make_async_copy(lab_hbm, lab, load_sem.at[0])
    load_x = pltpu.make_async_copy(x_hbm, xin, load_sem.at[1])
    load_lab.start()
    load_x.start()

    def place(j):
        n = j // 4
        dz = jnp.where(n % 2 == 1, 8 + (n + 1) // 2, 8 - n // 2)
        tz, ty = (z + dz) % 16, (y + j + 1) % 4
        tzl, tf = tz % 4, (tz // 4) * 4 + ty
        return tf, tzl * 8 + p % 8, tzl * 16 + tf

    barrier = pltpu.get_barrier_semaphore()

    def greet(tf, tp):
        pl.semaphore_signal(barrier, inc=1, device_id={"frame": tf, "pix": tp}, device_id_type=MESH)

    def greet_step(j, carry):
        tf, tp, _ = place(j)
        greet(tf, tp)
        return carry

    lax.fori_loop(0, 63, greet_step, 0)
    other_core = zl * 8 + x * 2 + (1 - c)
    greet(f, other_core)
    for d in range(1, 4):
        greet(f, zl * 8 + ((x + d) % 4) * 2 + c)
    for b in range(2):
        for xs in range(4):
            sf, sp = (2 * p + b) % 16, zl * 8 + xs * 2 + f % 2
            pl.when(jnp.logical_or(sf != f, sp != p))(lambda: greet(sf, sp))

    load_lab.wait()
    slot_sources(lab, onehot, weighted, ranked, cum, idx)
    load_x.wait()
    for i in range(64):
        a = (xin[0:16, pl.ds(i * 128, 128)].astype(F32) * 2048.0).astype(I32)
        b = (xin[16:32, pl.ds(i * 128, 128)].astype(F32) * 2048.0).astype(I32)
        src[pl.ds(i * 16, 16), :] = a + b * 65536

    pl.semaphore_wait(barrier, 75 - to_self.astype(I32))

    def pack(r, j):
        tile = jnp.broadcast_to(idx[pl.ds(r, 1), :], (8, 128))
        lane = jnp.broadcast_to(idx[pl.ds(64 + r, 1), :], (8, 128))
        upper = jnp.zeros((8, 128), I32)
        lower = jnp.zeros((8, 128), I32)
        for i in range(64):
            here = tile == i + 1
            up = jnp.take_along_axis(src[pl.ds(i * 16, 8), :], lane, axis=1, mode="promise_in_bounds")
            low = jnp.take_along_axis(src[pl.ds(i * 16 + 8, 8), :], lane, axis=1, mode="promise_in_bounds")
            upper = jnp.where(here, up, upper)
            lower = jnp.where(here, low, lower)
        pair = jnp.concatenate([upper, lower], axis=0)
        packed[j, 0:16, :] = ((pair & 0xFFFF).astype(F32) * (1 / 2048)).astype(BF16)
        packed[j, 16:32, :] = ((pair >> 16).astype(F32) * (1 / 2048)).astype(BF16)

    def send_step(j, carry):
        tf, tp, r = place(j)
        pack(r, j)
        pltpu.make_async_remote_copy(
            src_ref=packed.at[j],
            dst_ref=met.at[zl, pl.ds(pl.multiple_of(f * 32, 32), 32), :],
            send_sem=send_sem,
            recv_sem=met_sem,
            device_id={"frame": tf, "pix": tp},
            device_id_type=MESH,
        ).start()
        return carry

    lax.fori_loop(0, 63, send_step, 0)
    pack(own_bin, 63)
    pltpu.make_async_copy(
        packed.at[63], met.at[zl, pl.ds(pl.multiple_of(f * 32, 32), 32), :], met_sem
    ).start()
    pltpu.make_async_copy(met, met, met_sem).wait()

    right = jnp.concatenate([met[k] for k in range(4)], axis=1)
    valid = (right[0:16, :].astype(F32) > 0.0).astype(F32)
    valid = jnp.broadcast_to(valid[0:1, :], (16, 512))
    contract = (((1,), (1,)), ((), ()))

    def rows_of(parity):
        blocks = [pl.ds(pl.multiple_of((2 * i + parity) * 32, 32), 32) for i in range(8)]
        return jnp.concatenate(
            [jnp.concatenate([met[k, b, :] for b in blocks], axis=0) for k in range(4)], axis=1
        )

    part[0:256, :] = lax.dot_general(rows_of(1 - c), right, contract, preferred_element_type=F32)
    totals = lax.dot_general(valid.astype(BF16), right, contract, preferred_element_type=F32)[0:8]
    count = jnp.broadcast_to(jnp.sum(valid[0:8], axis=1, keepdims=True), (8, 512))
    part[256:264, :] = totals
    part[264:272, :] = count
    to_core = pltpu.make_async_remote_copy(
        src_ref=part, dst_ref=got, send_sem=core_send, recv_sem=core_recv,
        device_id={"frame": f, "pix": other_core}, device_id_type=MESH,
    )
    to_core.start()
    mine = lax.dot_general(rows_of(c), right, contract, preferred_element_type=F32)
    for b in range(4):
        half[b, 0:256, :] = mine[:, b * 128 : b * 128 + 128]
    to_core.wait()
    totals = totals + got[256:264, :]
    count = count[:, 0:128] + got[264:272, 0:128]
    for b in range(4):
        half[b, 0:256, :] = half[b, 0:256, :] + got[0:256, b * 128 : b * 128 + 128]
        for k in range(4):
            half[b, 256 + 8 * k : 264 + 8 * k, :] = totals[:, k * 128 : k * 128 + 128]
        half[b, 288:296, :] = count

    to_x = []
    for d in (2, 1, 3):
        tx = (x + d) % 4
        copy = pltpu.make_async_remote_copy(
            src_ref=half.at[tx], dst_ref=xgot.at[d - 1], send_sem=x_send.at[d - 1], recv_sem=x_recv.at[d - 1],
            device_id={"frame": f, "pix": zl * 8 + tx * 2 + c}, device_id_type=MESH,
        )
        copy.start()
        to_x.append(copy)
    for copy in to_x:
        copy.wait_recv()

    def summed(rows):
        return (half[x, rows, :] + xgot[0, rows, :]) + (xgot[1, rows, :] + xgot[2, rows, :])

    count = summed(pl.ds(288, 8))
    for b in range(4):
        inverse = 1.0 / summed(pl.ds(256 + 8 * b, 8))
        tcol[pl.ds(b * 128, 128), :] = jnp.broadcast_to(inverse[0:1, :], (128, 128)).T
    per_column = count / summed(pl.ds(pl.multiple_of(256 + 8 * x, 8), 8))
    per_column = jnp.broadcast_to(per_column[0:1, :], (32, 128))
    slot = own_bin % 2
    here = pl.ds(pl.multiple_of(x * 128, 128), 128)
    for i in range(8):
        tf = 2 * i + c
        rows = pl.ds(pl.multiple_of(tf * 32, 32), 32)
        fin[i] = summed(pl.ds(i * 32, 32)) * (per_column * tcol[rows, :])
        is_self = jnp.logical_and(tf == f, owner_p == p)

        @pl.when(is_self)
        def _():
            pltpu.make_async_copy(fin.at[i], out.at[slot, :, here], fin_recv).start()

        @pl.when(jnp.logical_not(is_self))
        def _():
            pltpu.make_async_remote_copy(
                src_ref=fin.at[i], dst_ref=out.at[slot, :, here], send_sem=fin_send, recv_sem=fin_recv,
                device_id={"frame": tf, "pix": owner_p}, device_id_type=MESH,
            ).start()

    pltpu.make_async_copy(out, out, fin_recv).wait()
    o_ref[...] = out[...]
    for copy in to_x:
        copy.wait_send()
    sent = packed.at[pl.ds(0, 63)]
    pltpu.make_async_copy(sent, sent, send_sem).wait()

    @pl.when(to_self)
    def _():
        some = fin.at[pl.ds(0, 7)]
        pltpu.make_async_copy(some, some, fin_send).wait()

    @pl.when(jnp.logical_not(to_self))
    def _():
        pltpu.make_async_copy(fin, fin, fin_send).wait()


def body(intensity, labels):
    dma = pltpu.SemaphoreType.DMA
    return pl.pallas_call(
        kernel,
        out_shape=jax.ShapeDtypeStruct((2, 32, 512), F32),
        in_specs=[pl.BlockSpec(memory_space=pl.ANY)] * 2,
        out_specs=pl.BlockSpec(memory_space=pltpu.VMEM),
        scratch_shapes=[
            pltpu.VMEM((64, 128), I32),
            pltpu.VMEM((32, 8192), BF16),
            pltpu.VMEM((4096, 128), BF16),
            pltpu.VMEM((128, 8192), BF16),
            pltpu.VMEM((128, 8192), BF16),
            pltpu.VMEM((4096, 256), F32),
            pltpu.VMEM((128, 128), I32),
            pltpu.VMEM((1024, 128), I32),
            pltpu.VMEM((64, 32, 128), BF16),
            pltpu.VMEM((4, 512, 128), BF16),
            pltpu.VMEM((272, 512), F32),
            pltpu.VMEM((272, 512), F32),
            pltpu.VMEM((4, MSG, 128), F32),
            pltpu.VMEM((3, MSG, 128), F32),
            pltpu.VMEM((512, 128), F32),
            pltpu.VMEM((8, 32, 128), F32),
            pltpu.VMEM((2, 32, 512), F32),
            dma((2,)), dma, dma, dma, dma, dma((3,)), dma((3,)), dma, dma,
        ],
        compiler_params=pltpu.CompilerParams(
            collective_id=0, has_side_effects=True, vmem_limit_bytes=32 << 20
        ),
        name="two_time",
    )(labels.reshape(64, 128), intensity)


def solution(mesh):
    return jax.shard_map(
        body,
        mesh=mesh,
        in_specs=(P("frame", "pix"), P("pix")),
        out_specs=P("pix", "frame", None),
        check_vma=False,
    )
```

```python
import jax
import jax.numpy as jnp
from jax import lax
from jax.experimental import pallas as pl
from jax.experimental.pallas import tpu as pltpu
from jax.sharding import PartitionSpec as P

MESH = pl.DeviceIdType.MESH
BF16, F32, I32 = jnp.bfloat16, jnp.float32, jnp.int32
LAG_X, LAG_Y = 4, 6


def iota(shape, dim):
    return lax.broadcasted_iota(I32, shape, dim)


def slot_sources(lab, onehot, weighted, ranked, cum, idx):
    bins = iota((64, 128), 0)
    lane = iota((64, 128), 1).astype(F32)
    for i in range(64):
        member = (lab[i : i + 1, :] == bins).astype(F32)
        onehot[pl.ds(i * 64, 64), :] = member.astype(BF16)
        weighted[0:64, pl.ds(i * 128, 128)] = (member * (i + 1.0)).astype(BF16)
        weighted[64:128, pl.ds(i * 128, 128)] = (member * lane).astype(BF16)
    row, col = iota((128, 256), 0), iota((128, 256), 1)
    upto = ((row <= col) | (col >= 128)).astype(F32).astype(BF16)
    cum[...] = jnp.dot(onehot[...], upto, preferred_element_type=F32)
    before = jnp.zeros((64, 128), F32)
    slot = iota((128, 128), 0).astype(F32)
    for i in range(64):
        member = onehot[pl.ds(i * 64, 64), :].astype(F32)
        through = cum[pl.ds(i * 64, 64), 0:128] + before
        rank = jnp.sum(member * through, axis=0, keepdims=True) - 1.0
        before = before + cum[pl.ds(i * 64, 64), 128:256]
        ranked[:, pl.ds(i * 128, 128)] = (slot == rank).astype(F32).astype(BF16)
    found = lax.dot_general(
        weighted[...], ranked[...], (((1,), (1,)), ((), ())), preferred_element_type=F32
    )
    idx[...] = found.astype(I32)


def kernel(
    lab_hbm, x_hbm, o_ref,
    lab, xin, onehot, weighted, ranked, cum, idx, src, packed, land, met, acc, got, tcol, fin, out,
    load_sem, z_send, z_recv, x_send, x_recv, y_send, y_recv, core_send, core_recv, fin_send, fin_recv,
):
    f, p = lax.axis_index("frame"), lax.axis_index("pix")
    zh, y = f // 4, f % 4
    zl, x, c = p // 8, (p // 2) % 4, p % 2
    z = zh * 4 + zl
    owner_c = zh // 2
    to_self = jnp.logical_and(zh % 2 == c, owner_c == c)

    load_lab = pltpu.make_async_copy(lab_hbm, lab, load_sem.at[0])
    load_x = pltpu.make_async_copy(x_hbm, xin, load_sem.at[1])
    load_lab.start()
    load_x.start()

    def along_z(dz):
        tz = lax.rem(z + dz, 16)
        return {"frame": lax.div(tz, 4) * 4 + y, "pix": lax.rem(tz, 4) * 8 + x * 2 + c}

    def along_x(tx):
        return {"frame": f, "pix": zl * 8 + tx * 2 + c}

    def along_y(ty):
        return {"frame": zh * 4 + ty, "pix": p}

    other_core = {"frame": f, "pix": zl * 8 + x * 2 + (1 - c)}

    barrier = pltpu.get_barrier_semaphore()

    def greet(device):
        pl.semaphore_signal(barrier, inc=1, device_id=device, device_id_type=MESH)

    for d in range(1, 16):
        greet(along_z(d))
    for d in range(1, 4):
        greet(along_x(lax.rem(x + d, 4)))
        greet(along_y(lax.rem(y + d, 4)))
    greet(other_core)
    for s in range(2):
        sender_zh, sender_c = 2 * c + s, zh % 2
        sender = {"frame": sender_zh * 4 + y, "pix": zl * 8 + x * 2 + sender_c}
        pl.when(jnp.logical_or(sender_zh != zh, sender_c != c))(lambda: greet(sender))

    load_lab.wait()
    slot_sources(lab, onehot, weighted, ranked, cum, idx)
    load_x.wait()
    for i in range(64):
        a = (xin[0:16, pl.ds(i * 128, 128)].astype(F32) * 2048.0).astype(I32)
        b = (xin[16:32, pl.ds(i * 128, 128)].astype(F32) * 2048.0).astype(I32)
        src[pl.ds(i * 16, 16), :] = a + b * 65536

    pl.semaphore_wait(barrier, 24 - to_self.astype(I32))

    def pack(r, slot, b):
        tile = jnp.broadcast_to(idx[pl.ds(r, 1), :], (8, 128))
        lane = jnp.broadcast_to(idx[pl.ds(64 + r, 1), :], (8, 128))
        upper = jnp.zeros((8, 128), I32)
        lower = jnp.zeros((8, 128), I32)
        for i in range(64):
            here = tile == i + 1
            up = jnp.take_along_axis(src[pl.ds(i * 16, 8), :], lane, axis=1, mode="promise_in_bounds")
            low = jnp.take_along_axis(src[pl.ds(i * 16 + 8, 8), :], lane, axis=1, mode="promise_in_bounds")
            upper = jnp.where(here, up, upper)
            lower = jnp.where(here, low, lower)
        pair = jnp.concatenate([upper, lower], axis=0)
        packed[slot, b, 0:16, :] = ((pair & 0xFFFF).astype(F32) * (1 / 2048)).astype(BF16)
        packed[slot, b, 16:32, :] = ((pair >> 16).astype(F32) * (1 / 2048)).astype(BF16)

    def slot_of(n):
        residue = lax.rem(4 - lax.div(n, 4), 4)
        return residue * 4 + lax.rem(6 - lax.rem(n, 4), 4)

    def depart(n):
        slot = slot_of(n)
        dz = lax.rem(slot, 4) * 4 + lax.div(slot, 4)
        tz = lax.rem(z + dz, 16)
        first = lax.rem(tz, 4) * 16 + lax.div(tz, 4)

        def one(b, carry):
            pack(first + 4 * b, slot, b)
            return carry

        lax.fori_loop(0, 4, one, 0)

        @pl.when(dz != 0)
        def _():
            pltpu.make_async_remote_copy(
                src_ref=packed.at[slot], dst_ref=land.at[slot], send_sem=z_send, recv_sem=z_recv.at[slot],
                device_id=along_z(dz), device_id_type=MESH,
            ).start()

        @pl.when(dz == 0)
        def _():
            pltpu.make_async_copy(packed.at[slot], land.at[slot], z_recv.at[slot]).start()

    def forward_x(n):
        slot = slot_of(n)
        pltpu.make_async_copy(land.at[slot], land.at[slot], z_recv.at[slot]).wait()
        for d in (2, 1, 3):
            tx = lax.rem(x + d, 4)
            pltpu.make_async_remote_copy(
                src_ref=land.at[slot, tx], dst_ref=met.at[slot, y, x], send_sem=x_send, recv_sem=x_recv.at[slot],
                device_id=along_x(tx), device_id_type=MESH,
            ).start()
        pltpu.make_async_copy(land.at[slot, x], met.at[slot, y, x], x_recv.at[slot]).start()

    def forward_y(n):
        slot = slot_of(n)
        pltpu.make_async_copy(met.at[slot, y], met.at[slot, y], x_recv.at[slot]).wait()
        for d in (2, 1, 3):
            pltpu.make_async_remote_copy(
                src_ref=met.at[slot, y], dst_ref=met.at[slot, y], send_sem=y_send, recv_sem=y_recv.at[lax.div(slot, 4)],
                device_id=along_y(lax.rem(y + d, 4)), device_id_type=MESH,
            ).start()

    def multiply(residue):
        group = met.at[pl.ds(residue * 4, 4), pl.ds(0, 3)]
        pltpu.make_async_copy(group, group, y_recv.at[residue]).wait()
        source_zl = lax.rem(zl + 4 - residue, 4)

        def slot(source_zh):
            return residue * 4 + lax.div(lax.rem(z + 16 - (source_zh * 4 + source_zl), 16), 4)

        slots = [slot(k) for k in range(4)]
        right = jnp.concatenate(
            [
                jnp.concatenate([met[s, ys, xs] for s in slots for ys in range(4)], axis=0)
                for xs in range(4)
            ],
            axis=1,
        )
        valid = (right[0:16, :].astype(F32) > 0.0).astype(F32)
        valid = jnp.broadcast_to(valid[0:1, :], (16, 512))

        def rows(source_zh):
            s = slot(source_zh)
            return jnp.concatenate([met[s, y, xs] for xs in range(4)], axis=1)

        left = jnp.concatenate(
            [rows(1 - c), rows(3 - c), valid.astype(BF16), rows(c), rows(2 + c)], axis=0
        )
        product = lax.dot_general(left, right, (((1,), (1,)), ((), ())), preferred_element_type=F32)
        if residue == 0:
            acc[...] = product
            acc[72:80, :] = valid[0:8, :]
        else:
            acc[0:72, :] = acc[0:72, :] + product[0:72, :]
            acc[72:80, :] = acc[72:80, :] + valid[0:8, :]
            acc[80:144, :] = acc[80:144, :] + product[80:144, :]

    def step(n, carry):
        pl.when(n < 16)(lambda: depart(n))
        pl.when(jnp.logical_and(n >= LAG_X, n < 16 + LAG_X))(lambda: forward_x(n - LAG_X))
        pl.when(jnp.logical_and(n >= LAG_Y, n < 16 + LAG_Y))(lambda: forward_y(n - LAG_Y))
        return carry

    done = 0
    for g in range(3):
        until = 4 * g + 5 + LAG_Y
        lax.fori_loop(done, until, step, 0)
        multiply((4 - g) % 4)
        done = until
    lax.fori_loop(done, 16 + LAG_Y, step, 0)
    multiply(1)

    acc[72:80, :] = jnp.broadcast_to(jnp.sum(acc[72:80, :], axis=1, keepdims=True), (8, 512))
    to_core = pltpu.make_async_remote_copy(
        src_ref=acc.at[pl.ds(0, 80)], dst_ref=got, send_sem=core_send, recv_sem=core_recv,
        device_id=other_core, device_id_type=MESH,
    )
    to_core.start()
    to_core.wait()
    totals = acc[64:72, :] + got[64:72, :]
    count = acc[72:80, :] + got[72:80, :]
    got[64:72, :] = 1.0 / totals
    per_column = jnp.broadcast_to((count / totals)[0:1, :], (32, 512))
    for k in range(2):
        target_zh = c + 2 * k
        inverse = got[64:72, pl.ds(pl.multiple_of(target_zh * 128, 128), 128)]
        tcol[...] = jnp.broadcast_to(inverse[0:1, :], (128, 128)).T
        per_row = tcol[pl.ds(pl.multiple_of(y * 32, 32), 32), :]
        per_row = jnp.concatenate([per_row] * 4, axis=1)
        whole = acc[80 + 32 * k : 112 + 32 * k, :] + got[32 * k : 32 * k + 32, :]
        fin[k] = whole * (per_column * per_row)
        is_self = jnp.logical_and(target_zh == zh, owner_c == c)

        @pl.when(is_self)
        def _():
            pltpu.make_async_copy(fin.at[k], out.at[zh % 2], fin_recv).start()

        @pl.when(jnp.logical_not(is_self))
        def _():
            pltpu.make_async_remote_copy(
                src_ref=fin.at[k], dst_ref=out.at[zh % 2], send_sem=fin_send, recv_sem=fin_recv,
                device_id={"frame": target_zh * 4 + y, "pix": zl * 8 + x * 2 + owner_c}, device_id_type=MESH,
            ).start()

    def wait_bytes(ref, sem):
        pltpu.make_async_copy(ref, ref, sem).wait()

    wait_bytes(packed.at[pl.ds(0, 15)], z_send)
    wait_bytes(land.at[:, pl.ds(0, 3)], x_send)
    wait_bytes(met.at[:, pl.ds(0, 3)], y_send)
    wait_bytes(out, fin_recv)
    o_ref[...] = out[...]
    pl.when(to_self)(lambda: wait_bytes(fin.at[0], fin_send))
    pl.when(jnp.logical_not(to_self))(lambda: wait_bytes(fin, fin_send))


def body(intensity, labels):
    dma = pltpu.SemaphoreType.DMA
    return pl.pallas_call(
        kernel,
        out_shape=jax.ShapeDtypeStruct((2, 32, 512), F32),
        in_specs=[pl.BlockSpec(memory_space=pl.ANY)] * 2,
        out_specs=pl.BlockSpec(memory_space=pltpu.VMEM),
        scratch_shapes=[
            pltpu.VMEM((64, 128), I32),
            pltpu.VMEM((32, 8192), BF16),
            pltpu.VMEM((4096, 128), BF16),
            pltpu.VMEM((128, 8192), BF16),
            pltpu.VMEM((128, 8192), BF16),
            pltpu.VMEM((4096, 256), F32),
            pltpu.VMEM((128, 128), I32),
            pltpu.VMEM((1024, 128), I32),
            pltpu.VMEM((16, 4, 32, 128), BF16),
            pltpu.VMEM((16, 4, 32, 128), BF16),
            pltpu.VMEM((16, 4, 4, 32, 128), BF16),
            pltpu.VMEM((144, 512), F32),
            pltpu.VMEM((80, 512), F32),
            pltpu.VMEM((128, 128), F32),
            pltpu.VMEM((2, 32, 512), F32),
            pltpu.VMEM((2, 32, 512), F32),
            dma((2,)), dma, dma((16,)), dma, dma((16,)), dma, dma((4,)), dma, dma, dma, dma,
        ],
        compiler_params=pltpu.CompilerParams(
            collective_id=0, has_side_effects=True, vmem_limit_bytes=60 << 20
        ),
        name="two_time",
    )(labels.reshape(64, 128), intensity)


def solution(mesh):
    return jax.shard_map(
        body,
        mesh=mesh,
        in_specs=(P("frame", "pix"), P("pix")),
        out_specs=P("pix", "frame", None),
        check_vma=False,
    )
```

```python
import jax
import jax.numpy as jnp
from jax import lax
from jax.experimental import pallas as pl
from jax.experimental.pallas import tpu as pltpu
from jax.sharding import PartitionSpec as P

MESH = pl.DeviceIdType.MESH
BF16, F32, I32 = jnp.bfloat16, jnp.float32, jnp.int32


def iota(shape, dim):
    return lax.broadcasted_iota(I32, shape, dim)


def slot_sources(lab, onehot, weighted, ranked, cum, idx):
    bins = iota((64, 128), 0)
    lane = iota((64, 128), 1).astype(F32)
    for i in range(64):
        member = (lab[i : i + 1, :] == bins).astype(F32)
        onehot[pl.ds(i * 64, 64), :] = member.astype(BF16)
        weighted[0:64, pl.ds(i * 128, 128)] = (member * (i + 1.0)).astype(BF16)
        weighted[64:128, pl.ds(i * 128, 128)] = (member * lane).astype(BF16)
    row, col = iota((128, 256), 0), iota((128, 256), 1)
    upto = ((row <= col) | (col >= 128)).astype(F32).astype(BF16)
    cum[...] = jnp.dot(onehot[...], upto, preferred_element_type=F32)
    before = jnp.zeros((64, 128), F32)
    slot = iota((128, 128), 0).astype(F32)
    for i in range(64):
        member = onehot[pl.ds(i * 64, 64), :].astype(F32)
        through = cum[pl.ds(i * 64, 64), 0:128] + before
        rank = jnp.sum(member * through, axis=0, keepdims=True) - 1.0
        before = before + cum[pl.ds(i * 64, 64), 128:256]
        ranked[:, pl.ds(i * 128, 128)] = (slot == rank).astype(F32).astype(BF16)
    found = lax.dot_general(
        weighted[...], ranked[...], (((1,), (1,)), ((), ())), preferred_element_type=F32
    )
    idx[...] = found.astype(I32)


def kernel(
    lab_hbm, x_hbm, o_ref,
    lab, xin, onehot, weighted, ranked, cum, idx, src, packed, land, met, acc, got, half, xgot, tcol, fin, out,
    load_sem, z_send, z_recv, y_send, y_recv, core_send, core_recv, x_send, x_recv, fin_send, fin_recv,
):
    f, p = lax.axis_index("frame"), lax.axis_index("pix")
    zh, y = f // 4, f % 4
    zl, x, c = p // 8, (p // 2) % 4, p % 2
    z = zh * 4 + zl
    pair, h = y // 2, y % 2
    owner_c = zh // 2
    row_y = h + 2 * c
    to_self = jnp.logical_and(jnp.logical_and(row_y == y, owner_c == c), x % 2 == pair)

    load_lab = pltpu.make_async_copy(lab_hbm, lab, load_sem.at[0])
    load_x = pltpu.make_async_copy(x_hbm, xin, load_sem.at[1])
    load_lab.start()
    load_x.start()

    def along_z(dz):
        tz = lax.rem(z + dz, 16)
        return {"frame": lax.div(tz, 4) * 4 + y, "pix": lax.rem(tz, 4) * 8 + x * 2 + c}

    def along_x(tx):
        return {"frame": f, "pix": zl * 8 + tx * 2 + c}

    def along_y(ty):
        return {"frame": zh * 4 + ty, "pix": p}

    other_core = {"frame": f, "pix": zl * 8 + x * 2 + (1 - c)}

    barrier = pltpu.get_barrier_semaphore()

    def greet(device):
        pl.semaphore_signal(barrier, inc=1, device_id=device, device_id_type=MESH)

    for d in range(1, 16):
        greet(along_z(d))
    for d in range(1, 4):
        greet(along_y(lax.rem(y + d, 4)))
        greet(along_x(lax.rem(x + d, 4)))
    greet(other_core)
    for s in range(2):
        for sx in range(4):
            szh, sy, sc = 2 * c + s, 2 * (x % 2) + h, pair
            same = jnp.logical_and(jnp.logical_and(szh == zh, sy == y), jnp.logical_and(sx == x, sc == c))
            sender = {"frame": szh * 4 + sy, "pix": zl * 8 + sx * 2 + sc}
            pl.when(jnp.logical_not(same))(lambda: greet(sender))

    load_lab.wait()
    slot_sources(lab, onehot, weighted, ranked, cum, idx)
    load_x.wait()
    for i in range(64):
        a = (xin[0:16, pl.ds(i * 128, 128)].astype(F32) * 2048.0).astype(I32)
        b = (xin[16:32, pl.ds(i * 128, 128)].astype(F32) * 2048.0).astype(I32)
        src[pl.ds(i * 16, 16), :] = a + b * 65536

    pl.semaphore_wait(barrier, 30 - to_self.astype(I32))

    def pack(r, wave, n, b):
        tile = jnp.broadcast_to(idx[pl.ds(r, 1), :], (8, 128))
        lane = jnp.broadcast_to(idx[pl.ds(64 + r, 1), :], (8, 128))
        upper = jnp.zeros((8, 128), I32)
        lower = jnp.zeros((8, 128), I32)
        for i in range(64):
            here = tile == i + 1
            up = jnp.take_along_axis(src[pl.ds(i * 16, 8), :], lane, axis=1, mode="promise_in_bounds")
            low = jnp.take_along_axis(src[pl.ds(i * 16 + 8, 8), :], lane, axis=1, mode="promise_in_bounds")
            upper = jnp.where(here, up, upper)
            lower = jnp.where(here, low, lower)
        pair_of = jnp.concatenate([upper, lower], axis=0)
        packed[wave, n, b, 0:16, :] = ((pair_of & 0xFFFF).astype(F32) * (1 / 2048)).astype(BF16)
        packed[wave, n, b, 16:32, :] = ((pair_of >> 16).astype(F32) * (1 / 2048)).astype(BF16)

    def depart(t, carry):
        wave, n = lax.div(t, 16), lax.rem(t, 16)
        dz = lax.rem(8 + jnp.where(lax.rem(n, 2) == 1, lax.div(n + 1, 2), 16 - lax.div(n, 2)), 16)
        tz = lax.rem(z + dz, 16)
        first = lax.rem(tz, 4) * 16 + lax.div(tz, 4) + 8 * wave

        def one(b, carry):
            pack(first + 4 * b, wave, n, b)
            return carry

        lax.fori_loop(0, 2, one, 0)
        done = z_recv.at[wave, lax.div(n, 4)]

        @pl.when(n < 15)
        def _():
            pltpu.make_async_remote_copy(
                src_ref=packed.at[wave, n], dst_ref=land.at[wave, n], send_sem=z_send, recv_sem=done,
                device_id=along_z(dz), device_id_type=MESH,
            ).start()

        @pl.when(n == 15)
        def _():
            pltpu.make_async_copy(packed.at[wave, n], land.at[wave, n], done).start()

        return carry

    lax.fori_loop(0, 32, depart, 0)

    def forward(wave, k):
        steps = pl.ds(4 * k, 4)
        arrived = land.at[wave, steps]
        pltpu.make_async_copy(arrived, arrived, z_recv.at[wave, k]).wait()
        to = met.at[wave, steps, y]
        for b, ty in ((1 - pair, 2 - 2 * pair), (1 - pair, 3 - 2 * pair), (pair, 2 * pair + 1 - h)):
            pltpu.make_async_remote_copy(
                src_ref=land.at[wave, steps, b], dst_ref=to, send_sem=y_send, recv_sem=y_recv.at[wave],
                device_id=along_y(ty), device_id_type=MESH,
            ).start()
        pltpu.make_async_copy(land.at[wave, steps, pair], to, y_recv.at[wave]).start()

    def step_from(source_z):
        dz = lax.rem(z + 16 - source_z, 16)
        return jnp.where(dz == 0, 15, jnp.where(dz <= 8, 16 - 2 * dz, 2 * dz - 17))

    steps = [[step_from(4 * k + m) for k in range(4)] for m in range(4)]

    def multiply(wave):
        pltpu.make_async_copy(met.at[wave], met.at[wave], y_recv.at[wave]).wait()

        def frames(ys):
            return jnp.concatenate(
                [
                    jnp.concatenate([met[wave, steps[m][k], v] for k in range(4) for v in ys], axis=0)
                    for m in range(4)
                ],
                axis=1,
            )

        right = frames(range(4))
        valid = (right[0:16, :].astype(F32) > 0.0).astype(F32)
        valid = jnp.broadcast_to(valid[0:1, :], (16, 512))
        left = jnp.concatenate(
            [frames([h + 2 - 2 * c]), valid.astype(BF16), frames([row_y])], axis=0
        )
        acc[wave] = lax.dot_general(left, right, (((1,), (1,)), ((), ())), preferred_element_type=F32)
        acc[wave, 136:144, :] = jnp.broadcast_to(
            jnp.sum(valid[0:8], axis=1, keepdims=True), (8, 512)
        )

    def core_copy(wave):
        return pltpu.make_async_remote_copy(
            src_ref=acc.at[wave, pl.ds(0, 144)], dst_ref=got.at[wave],
            send_sem=core_send.at[wave], recv_sem=core_recv.at[wave],
            device_id=other_core, device_id_type=MESH,
        )

    def x_copy(wave, d):
        tx = lax.rem(x + d, 4)
        return pltpu.make_async_remote_copy(
            src_ref=half.at[wave, tx], dst_ref=xgot.at[wave, d - 1],
            send_sem=x_send.at[wave, d - 1], recv_sem=x_recv.at[wave, d - 1],
            device_id=along_x(tx), device_id_type=MESH,
        )

    def add_cores(wave):
        core_copy(wave).wait()
        totals = acc[wave, 128:136, :] + got[wave, 128:136, :]
        count = acc[wave, 136:144, 0:128] + got[wave, 136:144, 0:128]
        for b in range(4):
            block = pl.ds(b * 128, 128)
            half[wave, b, 0:128, :] = acc[wave, 144:272, block] + got[wave, 0:128, block]
            for k in range(4):
                half[wave, b, 128 + 8 * k : 136 + 8 * k, :] = totals[:, k * 128 : k * 128 + 128]
            half[wave, b, 160:168, :] = count

    def finish(wave):
        for d in (2, 1, 3):
            x_copy(wave, d).wait_recv()

        def summed(rows):
            return (half[wave, x, rows, :] + xgot[wave, 0, rows, :]) + (
                xgot[wave, 1, rows, :] + xgot[wave, 2, rows, :]
            )

        per_column = summed(pl.ds(160, 8)) / summed(pl.ds(pl.multiple_of(128 + 8 * x, 8), 8))
        per_column = jnp.broadcast_to(per_column[0:1, :], (32, 128))
        here = pl.ds(pl.multiple_of(x * 128, 128), 128)
        owner_x = 2 * wave + pair
        for k in range(4):
            inverse = 1.0 / summed(pl.ds(128 + 8 * k, 8))
            tcol[k] = jnp.broadcast_to(inverse[0:1, :], (128, 128)).T
            per_row = tcol[k, pl.ds(pl.multiple_of(row_y * 32, 32), 32), :]
            fin[4 * wave + k] = summed(pl.ds(32 * k, 32)) * (per_column * per_row)
            is_self = jnp.logical_and(to_self, jnp.logical_and(zh == k, owner_x == x))

            @pl.when(is_self)
            def _():
                pltpu.make_async_copy(fin.at[4 * wave + k], out.at[zh % 2, :, here], fin_recv).start()

            @pl.when(jnp.logical_not(is_self))
            def _():
                pltpu.make_async_remote_copy(
                    src_ref=fin.at[4 * wave + k], dst_ref=out.at[zh % 2, :, here],
                    send_sem=fin_send, recv_sem=fin_recv,
                    device_id={"frame": k * 4 + row_y, "pix": zl * 8 + owner_x * 2 + owner_c},
                    device_id_type=MESH,
                ).start()

    for k in range(4):
        forward(0, k)
    multiply(0)
    core_copy(0).start()
    add_cores(0)
    for d in (2, 1, 3):
        x_copy(0, d).start()
    for k in range(2):
        forward(1, k)
    finish(0)
    for k in range(2, 4):
        forward(1, k)
    multiply(1)
    core_copy(1).start()
    add_cores(1)
    for d in (2, 1, 3):
        x_copy(1, d).start()
    finish(1)

    def wait_bytes(ref, sem):
        pltpu.make_async_copy(ref, ref, sem).wait()

    wait_bytes(packed.at[:, pl.ds(0, 15)], z_send)
    wait_bytes(met.at[:, :, pl.ds(0, 3)], y_send)
    for wave in range(2):
        for d in (2, 1, 3):
            x_copy(wave, d).wait_send()
    pl.when(to_self)(lambda: wait_bytes(fin.at[pl.ds(0, 7)], fin_send))
    pl.when(jnp.logical_not(to_self))(lambda: wait_bytes(fin, fin_send))
    wait_bytes(out, fin_recv)
    o_ref[...] = out[...]


def body(intensity, labels):
    dma = pltpu.SemaphoreType.DMA
    return pl.pallas_call(
        kernel,
        out_shape=jax.ShapeDtypeStruct((2, 32, 512), F32),
        in_specs=[pl.BlockSpec(memory_space=pl.ANY)] * 2,
        out_specs=pl.BlockSpec(memory_space=pltpu.VMEM),
        scratch_shapes=[
            pltpu.VMEM((64, 128), I32),
            pltpu.VMEM((32, 8192), BF16),
            pltpu.VMEM((4096, 128), BF16),
            pltpu.VMEM((128, 8192), BF16),
            pltpu.VMEM((128, 8192), BF16),
            pltpu.VMEM((4096, 256), F32),
            pltpu.VMEM((128, 128), I32),
            pltpu.VMEM((1024, 128), I32),
            pltpu.VMEM((2, 16, 2, 32, 128), BF16),
            pltpu.VMEM((2, 16, 2, 32, 128), BF16),
            pltpu.VMEM((2, 16, 4, 32, 128), BF16),
            pltpu.VMEM((2, 272, 512), F32),
            pltpu.VMEM((2, 144, 512), F32),
            pltpu.VMEM((2, 4, 168, 128), F32),
            pltpu.VMEM((2, 3, 168, 128), F32),
            pltpu.VMEM((4, 128, 128), F32),
            pltpu.VMEM((8, 32, 128), F32),
            pltpu.VMEM((2, 32, 512), F32),
            dma((2,)), dma, dma((2, 4)), dma, dma((2,)), dma((2,)), dma((2,)), dma((2, 3)), dma((2, 3)), dma, dma,
        ],
        compiler_params=pltpu.CompilerParams(
            collective_id=0, has_side_effects=True, vmem_limit_bytes=60 << 20
        ),
        name="two_time",
    )(labels.reshape(64, 128), intensity)


def solution(mesh):
    return jax.shard_map(
        body,
        mesh=mesh,
        in_specs=(P("frame", "pix"), P("pix")),
        out_specs=P("pix", "frame", None),
        check_vma=False,
    )
```

```python
import jax
import jax.numpy as jnp
from jax import lax
from jax.experimental import pallas as pl
from jax.experimental.pallas import tpu as pltpu
from jax.sharding import PartitionSpec as P

MESH = pl.DeviceIdType.MESH
BF16, F32, I32 = jnp.bfloat16, jnp.float32, jnp.int32
MSG = 296


def iota(shape, dim):
    return lax.broadcasted_iota(I32, shape, dim)


def slot_sources(lab, onehot, weighted, ranked, cum, idx):
    bins = iota((64, 128), 0)
    lane = iota((64, 128), 1).astype(F32)
    for i in range(64):
        member = (lab[i : i + 1, :] == bins).astype(F32)
        onehot[pl.ds(i * 64, 64), :] = member.astype(BF16)
        weighted[0:64, pl.ds(i * 128, 128)] = (member * (i + 1.0)).astype(BF16)
        weighted[64:128, pl.ds(i * 128, 128)] = (member * lane).astype(BF16)
    row, col = iota((128, 256), 0), iota((128, 256), 1)
    upto = ((row <= col) | (col >= 128)).astype(F32).astype(BF16)
    cum[...] = jnp.dot(onehot[...], upto, preferred_element_type=F32)
    before = jnp.zeros((64, 128), F32)
    slot = iota((128, 128), 0).astype(F32)
    for i in range(64):
        member = onehot[pl.ds(i * 64, 64), :].astype(F32)
        through = cum[pl.ds(i * 64, 64), 0:128] + before
        rank = jnp.sum(member * through, axis=0, keepdims=True) - 1.0
        before = before + cum[pl.ds(i * 64, 64), 128:256]
        ranked[:, pl.ds(i * 128, 128)] = (slot == rank).astype(F32).astype(BF16)
    found = lax.dot_general(
        weighted[...], ranked[...], (((1,), (1,)), ((), ())), preferred_element_type=F32
    )
    idx[...] = found.astype(I32)


def kernel(
    lab_hbm, x_hbm, o_ref,
    lab, xin, onehot, weighted, ranked, cum, idx, src, packed, met, tot, tot_got, part, got, half, xgot, tcol, fin, out,
    load_sem, line_sem, sheet_sem, send_sem, met_sem, core_send, core_recv, x_send, x_recv, fin_send, fin_recv,
):
    f, p = lax.axis_index("frame"), lax.axis_index("pix")
    zh, y = f // 4, f % 4
    zl, x, c = p // 8, (p // 2) % 4, p % 2
    z = zh * 4 + zl
    own_bin = zl * 16 + y * 4 + zh
    owner_p = zl * 8 + y * 2 + zh // 2
    to_self = jnp.logical_and(owner_p == p, y % 2 == c)

    load_lab = pltpu.make_async_copy(lab_hbm, lab, load_sem.at[0])
    load_x = pltpu.make_async_copy(x_hbm, xin, load_sem.at[1])
    load_lab.start()
    load_x.start()

    def on_sheet(dy, dz):
        ty, tz = lax.rem(y + dy, 4), lax.rem(z + dz, 16)
        tzl, tzh = lax.rem(tz, 4), lax.div(tz, 4)
        return tzh * 4 + ty, tzl * 8 + x * 2 + c, tzl * 16 + ty * 4 + tzh

    def signal(sem, tf, tp):
        pl.semaphore_signal(sem, inc=1, device_id={"frame": tf, "pix": tp}, device_id_type=MESH)

    def beside(dx, dc):
        return zl * 8 + lax.rem(x + dx, 4) * 2 + (c if dc == 0 else 1 - c)

    others = [(dx, dc) for dx in range(4) for dc in range(2) if (dx, dc) != (0, 0)]
    other_core = beside(0, 1)

    barrier = pltpu.get_barrier_semaphore()
    for d in range(1, 16):
        signal(barrier, *on_sheet(0, d)[:2])
    for d in range(1, 4):
        signal(barrier, *on_sheet(d, 0)[:2])
    for dx, dc in others:
        signal(barrier, f, beside(dx, dc))

    load_lab.wait()
    slot_sources(lab, onehot, weighted, ranked, cum, idx)
    load_x.wait()
    for i in range(64):
        a = (xin[0:16, pl.ds(i * 128, 128)].astype(F32) * 2048.0).astype(I32)
        b = (xin[16:32, pl.ds(i * 128, 128)].astype(F32) * 2048.0).astype(I32)
        src[pl.ds(i * 16, 16), :] = a + b * 65536

    pl.semaphore_wait(barrier, 25)
    for d in range(1, 4):
        signal(line_sem, *on_sheet(d, 0)[:2])

    def pack(r, j):
        tile = jnp.broadcast_to(idx[pl.ds(r, 1), :], (8, 128))
        lane = jnp.broadcast_to(idx[pl.ds(64 + r, 1), :], (8, 128))
        upper = jnp.zeros((8, 128), I32)
        lower = jnp.zeros((8, 128), I32)
        for i in range(64):
            here = tile == i + 1
            up = jnp.take_along_axis(src[pl.ds(i * 16, 8), :], lane, axis=1, mode="promise_in_bounds")
            low = jnp.take_along_axis(src[pl.ds(i * 16 + 8, 8), :], lane, axis=1, mode="promise_in_bounds")
            upper = jnp.where(here, up, upper)
            lower = jnp.where(here, low, lower)
        pair = jnp.concatenate([upper, lower], axis=0)
        packed[j, 0:16, :] = ((pair & 0xFFFF).astype(F32) * (1 / 2048)).astype(BF16)
        packed[j, 16:32, :] = ((pair >> 16).astype(F32) * (1 / 2048)).astype(BF16)

    def send_step(j, carry):
        n = lax.rem(j, 16)
        dz = lax.rem(8 + jnp.where(lax.rem(n, 2) == 1, lax.div(n + 1, 2), 16 - lax.div(n, 2)), 16)
        tf, tp, r = on_sheet(lax.div(j, 16), dz)
        pack(r, j)
        pltpu.make_async_remote_copy(
            src_ref=packed.at[j],
            dst_ref=met.at[zl, pl.ds(pl.multiple_of(f * 32, 32), 32), :],
            send_sem=send_sem,
            recv_sem=met_sem,
            device_id={"frame": tf, "pix": tp},
            device_id_type=MESH,
        ).start()
        return carry

    lax.fori_loop(0, 15, send_step, 0)
    pack(own_bin, 15)
    pltpu.make_async_copy(
        packed.at[15], met.at[zl, pl.ds(pl.multiple_of(f * 32, 32), 32), :], met_sem
    ).start()
    pl.semaphore_wait(line_sem, 3)
    for dx, dc in others:
        signal(sheet_sem, f, beside(dx, dc))
    lax.fori_loop(16, 64, send_step, 0)
    pltpu.make_async_copy(met, met, met_sem).wait()

    right = jnp.concatenate([met[k] for k in range(4)], axis=1)
    valid = (right[0:16, :].astype(F32) > 0.0).astype(F32)
    valid = jnp.broadcast_to(valid[0:1, :], (16, 512))
    contract = (((1,), (1,)), ((), ()))

    def rows_of(parity):
        blocks = [pl.ds(pl.multiple_of((2 * i + parity) * 32, 32), 32) for i in range(8)]
        return jnp.concatenate(
            [jnp.concatenate([met[k, b, :] for b in blocks], axis=0) for k in range(4)], axis=1
        )

    totals = lax.dot_general(valid.astype(BF16), right, contract, preferred_element_type=F32)[0:8]
    for b in range(4):
        tot[8 * b : 8 * b + 8, :] = totals[:, b * 128 : b * 128 + 128]
    tot[32:40, :] = jnp.broadcast_to(jnp.sum(valid[0:8], axis=1, keepdims=True), (8, 128))
    theirs = lax.dot_general(rows_of(1 - c), right, contract, preferred_element_type=F32)
    for b in range(4):
        part[b] = theirs[:, b * 128 : b * 128 + 128]

    def core_copy(source, target, k):
        return pltpu.make_async_remote_copy(
            src_ref=source, dst_ref=target, send_sem=core_send.at[k], recv_sem=core_recv.at[k],
            device_id={"frame": f, "pix": other_core}, device_id_type=MESH,
        )

    to_core = [core_copy(tot, tot_got, 4)]
    order = [(d, lax.rem(x + d, 4)) for d in (2, 1, 3, 0)]
    to_core += [core_copy(part.at[b], got.at[b], d) for d, b in order]
    for copy in to_core:
        copy.start()
    mine = lax.dot_general(rows_of(c), right, contract, preferred_element_type=F32)
    for b in range(4):
        half[b, 0:256, :] = mine[:, b * 128 : b * 128 + 128]
    to_core[0].wait()
    both = tot[...] + tot_got[...]
    for b in range(4):
        half[b, 256:MSG, :] = both
    to_x = []
    for (d, b), copy in zip(order, to_core[1:]):
        copy.wait()
        half[b, 0:256, :] = half[b, 0:256, :] + got[b]
        if d != 0:
            copy = pltpu.make_async_remote_copy(
                src_ref=half.at[b], dst_ref=xgot.at[d - 1], send_sem=x_send.at[d - 1], recv_sem=x_recv.at[d - 1],
                device_id={"frame": f, "pix": beside(d, 0)}, device_id_type=MESH,
            )
            copy.start()
            to_x.append(copy)
    for copy in to_x:
        copy.wait_recv()
    pl.semaphore_wait(sheet_sem, 7)

    def summed(rows):
        return (half[x, rows, :] + xgot[0, rows, :]) + (xgot[1, rows, :] + xgot[2, rows, :])

    count = summed(pl.ds(288, 8))
    for b in range(4):
        inverse = 1.0 / summed(pl.ds(256 + 8 * b, 8))
        tcol[pl.ds(b * 128, 128), :] = jnp.broadcast_to(inverse[0:1, :], (128, 128)).T
    per_column = count / summed(pl.ds(pl.multiple_of(256 + 8 * x, 8), 8))
    per_column = jnp.broadcast_to(per_column[0:1, :], (32, 128))
    slot = zh % 2
    here = pl.ds(pl.multiple_of(x * 128, 128), 128)
    for i in range(8):
        tf = 2 * i + c
        rows = pl.ds(pl.multiple_of(tf * 32, 32), 32)
        fin[i] = summed(pl.ds(i * 32, 32)) * (per_column * tcol[rows, :])
        is_self = jnp.logical_and(tf == f, owner_p == p)

        @pl.when(is_self)
        def _():
            pltpu.make_async_copy(fin.at[i], out.at[slot, :, here], fin_recv).start()

        @pl.when(jnp.logical_not(is_self))
        def _():
            pltpu.make_async_remote_copy(
                src_ref=fin.at[i], dst_ref=out.at[slot, :, here], send_sem=fin_send, recv_sem=fin_recv,
                device_id={"frame": tf, "pix": owner_p}, device_id_type=MESH,
            ).start()

    pltpu.make_async_copy(out, out, fin_recv).wait()
    o_ref[...] = out[...]
    for copy in to_x:
        copy.wait_send()
    sent = packed.at[pl.ds(0, 63)]
    pltpu.make_async_copy(sent, sent, send_sem).wait()

    @pl.when(to_self)
    def _():
        some = fin.at[pl.ds(0, 7)]
        pltpu.make_async_copy(some, some, fin_send).wait()

    @pl.when(jnp.logical_not(to_self))
    def _():
        pltpu.make_async_copy(fin, fin, fin_send).wait()


def body(intensity, labels):
    dma = pltpu.SemaphoreType.DMA
    return pl.pallas_call(
        kernel,
        out_shape=jax.ShapeDtypeStruct((2, 32, 512), F32),
        in_specs=[pl.BlockSpec(memory_space=pl.ANY)] * 2,
        out_specs=pl.BlockSpec(memory_space=pltpu.VMEM),
        scratch_shapes=[
            pltpu.VMEM((64, 128), I32),
            pltpu.VMEM((32, 8192), BF16),
            pltpu.VMEM((4096, 128), BF16),
            pltpu.VMEM((128, 8192), BF16),
            pltpu.VMEM((128, 8192), BF16),
            pltpu.VMEM((4096, 256), F32),
            pltpu.VMEM((128, 128), I32),
            pltpu.VMEM((1024, 128), I32),
            pltpu.VMEM((64, 32, 128), BF16),
            pltpu.VMEM((4, 512, 128), BF16),
            pltpu.VMEM((40, 128), F32),
            pltpu.VMEM((40, 128), F32),
            pltpu.VMEM((4, 256, 128), F32),
            pltpu.VMEM((4, 256, 128), F32),
            pltpu.VMEM((4, MSG, 128), F32),
            pltpu.VMEM((3, MSG, 128), F32),
            pltpu.VMEM((512, 128), F32),
            pltpu.VMEM((8, 32, 128), F32),
            pltpu.VMEM((2, 32, 512), F32),
            dma((2,)), pltpu.SemaphoreType.REGULAR, pltpu.SemaphoreType.REGULAR, dma, dma,
            dma((5,)), dma((5,)), dma((3,)), dma((3,)), dma, dma,
        ],
        compiler_params=pltpu.CompilerParams(
            collective_id=0, has_side_effects=True, vmem_limit_bytes=60 << 20
        ),
        name="two_time",
    )(labels.reshape(64, 128), intensity)


def solution(mesh):
    return jax.shard_map(
        body,
        mesh=mesh,
        in_specs=(P("frame", "pix"), P("pix")),
        out_specs=P("pix", "frame", None),
        check_vma=False,
    )
```

```python
import jax
import jax.numpy as jnp
from jax import lax
from jax.experimental import pallas as pl
from jax.experimental.pallas import tpu as pltpu
from jax.sharding import PartitionSpec as P

MESH = pl.DeviceIdType.MESH
BF16, F32, I32 = jnp.bfloat16, jnp.float32, jnp.int32
MSG = 168


def iota(shape, dim):
    return lax.broadcasted_iota(I32, shape, dim)


def slot_sources(lab, onehot, weighted, ranked, cum, idx):
    bins = iota((64, 128), 0)
    lane = iota((64, 128), 1).astype(F32)
    for i in range(64):
        member = (lab[i : i + 1, :] == bins).astype(F32)
        onehot[pl.ds(i * 64, 64), :] = member.astype(BF16)
        weighted[0:64, pl.ds(i * 128, 128)] = (member * (i + 1.0)).astype(BF16)
        weighted[64:128, pl.ds(i * 128, 128)] = (member * lane).astype(BF16)
    row, col = iota((128, 256), 0), iota((128, 256), 1)
    upto = ((row <= col) | (col >= 128)).astype(F32).astype(BF16)
    cum[...] = jnp.dot(onehot[...], upto, preferred_element_type=F32)
    before = jnp.zeros((64, 128), F32)
    slot = iota((128, 128), 0).astype(F32)
    for i in range(64):
        member = onehot[pl.ds(i * 64, 64), :].astype(F32)
        through = cum[pl.ds(i * 64, 64), 0:128] + before
        rank = jnp.sum(member * through, axis=0, keepdims=True) - 1.0
        before = before + cum[pl.ds(i * 64, 64), 128:256]
        ranked[:, pl.ds(i * 128, 128)] = (slot == rank).astype(F32).astype(BF16)
    found = lax.dot_general(
        weighted[...], ranked[...], (((1,), (1,)), ((), ())), preferred_element_type=F32
    )
    idx[...] = found.astype(I32)


def kernel(
    lab_hbm, x_hbm, o_ref,
    lab, xin, onehot, weighted, ranked, cum, idx, src, packed, met, tot, tot_got, part, got, half, xgot, tcol, fin, out,
    load_sem, line_sem, sheet_sem, send_sem, met_sem, core_send, core_recv, x_send, x_recv, fin_send, fin_recv,
):
    f, p = lax.axis_index("frame"), lax.axis_index("pix")
    zh, y = f // 4, f % 4
    zl, x, c = p // 8, (p // 2) % 4, p % 2
    z = zh * 4 + zl
    own_bin = zl * 16 + y * 4 + zh
    owner_p = zl * 8 + y * 2 + zh // 2
    to_self = jnp.logical_and(owner_p == p, y % 2 == c)

    load_lab = pltpu.make_async_copy(lab_hbm, lab, load_sem.at[0])
    load_x = pltpu.make_async_copy(x_hbm, xin, load_sem.at[1])
    load_lab.start()
    load_x.start()

    def on_sheet(dy, dz):
        ty, tz = lax.rem(y + dy, 4), lax.rem(z + dz, 16)
        tzl, tzh = lax.rem(tz, 4), lax.div(tz, 4)
        return tzh * 4 + ty, tzl * 8 + x * 2 + c, tzl * 16 + ty * 4 + tzh

    def signal(sem, tf, tp):
        pl.semaphore_signal(sem, inc=1, device_id={"frame": tf, "pix": tp}, device_id_type=MESH)

    def beside(dx, dc):
        return zl * 8 + lax.rem(x + dx, 4) * 2 + (c if dc == 0 else 1 - c)

    others = [(dx, dc) for dx in range(4) for dc in range(2) if (dx, dc) != (0, 0)]
    other_core = beside(0, 1)

    barrier = pltpu.get_barrier_semaphore()
    for d in range(1, 16):
        signal(barrier, *on_sheet(0, d)[:2])
    for d in range(1, 4):
        signal(barrier, *on_sheet(d, 0)[:2])
    for dx, dc in others:
        signal(barrier, f, beside(dx, dc))

    load_lab.wait()
    slot_sources(lab, onehot, weighted, ranked, cum, idx)
    load_x.wait()
    for i in range(64):
        a = (xin[0:16, pl.ds(i * 128, 128)].astype(F32) * 2048.0).astype(I32)
        b = (xin[16:32, pl.ds(i * 128, 128)].astype(F32) * 2048.0).astype(I32)
        src[pl.ds(i * 16, 16), :] = a + b * 65536

    pl.semaphore_wait(barrier, 25)
    for d in range(1, 4):
        signal(line_sem, *on_sheet(d, 0)[:2])

    def pack(r, j):
        tile = jnp.broadcast_to(idx[pl.ds(r, 1), :], (8, 128))
        lane = jnp.broadcast_to(idx[pl.ds(64 + r, 1), :], (8, 128))
        upper = jnp.zeros((8, 128), I32)
        lower = jnp.zeros((8, 128), I32)
        for i in range(64):
            here = tile == i + 1
            up = jnp.take_along_axis(src[pl.ds(i * 16, 8), :], lane, axis=1, mode="promise_in_bounds")
            low = jnp.take_along_axis(src[pl.ds(i * 16 + 8, 8), :], lane, axis=1, mode="promise_in_bounds")
            upper = jnp.where(here, up, upper)
            lower = jnp.where(here, low, lower)
        pair = jnp.concatenate([upper, lower], axis=0)
        packed[j, 0:16, :] = ((pair & 0xFFFF).astype(F32) * (1 / 2048)).astype(BF16)
        packed[j, 16:32, :] = ((pair >> 16).astype(F32) * (1 / 2048)).astype(BF16)

    def send_step(j, carry):
        n = lax.rem(j, 16)
        dz = lax.rem(8 + jnp.where(lax.rem(n, 2) == 1, lax.div(n + 1, 2), 16 - lax.div(n, 2)), 16)
        tf, tp, r = on_sheet(lax.div(j, 16), dz)
        pack(r, j)
        pltpu.make_async_remote_copy(
            src_ref=packed.at[j],
            dst_ref=met.at[zl, pl.ds(pl.multiple_of(f * 32, 32), 32), :],
            send_sem=send_sem,
            recv_sem=met_sem,
            device_id={"frame": tf, "pix": tp},
            device_id_type=MESH,
        ).start()
        return carry

    lax.fori_loop(0, 15, send_step, 0)
    pack(own_bin, 15)
    pltpu.make_async_copy(
        packed.at[15], met.at[zl, pl.ds(pl.multiple_of(f * 32, 32), 32), :], met_sem
    ).start()
    pl.semaphore_wait(line_sem, 3)
    for dx, dc in others:
        signal(sheet_sem, f, beside(dx, dc))
    lax.fori_loop(16, 64, send_step, 0)
    pltpu.make_async_copy(met, met, met_sem).wait()

    right = jnp.concatenate([met[k] for k in range(4)], axis=1)
    valid = (right[0:16, :].astype(F32) > 0.0).astype(F32)
    valid = jnp.broadcast_to(valid[0:1, :], (16, 512))
    contract = (((1,), (1,)), ((), ()))

    def product(part_of, core):
        blocks = [pl.ds(pl.multiple_of((4 * k + 2 * part_of + core) * 32, 32), 32) for k in range(4)]
        left = jnp.concatenate(
            [jnp.concatenate([met[k, b, :] for b in blocks], axis=0) for k in range(4)], axis=1
        )
        return lax.dot_general(left, right, contract, preferred_element_type=F32)

    totals = lax.dot_general(valid.astype(BF16), right, contract, preferred_element_type=F32)[0:8]
    for b in range(4):
        tot[8 * b : 8 * b + 8, :] = totals[:, b * 128 : b * 128 + 128]
    tot[32:40, :] = jnp.broadcast_to(jnp.sum(valid[0:8], axis=1, keepdims=True), (8, 128))

    def core_copy(source, target, k):
        return pltpu.make_async_remote_copy(
            src_ref=source, dst_ref=target, send_sem=core_send.at[k], recv_sem=core_recv.at[k],
            device_id={"frame": f, "pix": other_core}, device_id_type=MESH,
        )

    order = [(d, lax.rem(x + d, 4)) for d in (2, 1, 3, 0)]
    to_core = [core_copy(tot, tot_got, 8)]
    to_core[0].start()
    for m in range(2):
        theirs = product(m, 1 - c)
        for b in range(4):
            part[m, b] = theirs[:, b * 128 : b * 128 + 128]
        for d, b in order:
            to_core.append(core_copy(part.at[m, b], got.at[m, b], 4 * m + d))
            to_core[-1].start()
    to_x = []
    for m in range(2):
        mine = product(m, c)
        for b in range(4):
            half[m, b, 0:128, :] = mine[:, b * 128 : b * 128 + 128]
        if m == 0:
            to_core[0].wait()
            both = tot[...] + tot_got[...]
            for b in range(4):
                half[0, b, 128:MSG, :] = both
        rows = pl.ds(0, 128 if m else MSG)
        for (d, b), copy in zip(order, to_core[1 + 4 * m : 5 + 4 * m]):
            copy.wait()
            half[m, b, 0:128, :] = half[m, b, 0:128, :] + got[m, b]
            if d != 0:
                copy = pltpu.make_async_remote_copy(
                    src_ref=half.at[m, b, rows], dst_ref=xgot.at[m, d - 1, rows],
                    send_sem=x_send.at[m, d - 1], recv_sem=x_recv.at[m, d - 1],
                    device_id={"frame": f, "pix": beside(d, 0)}, device_id_type=MESH,
                )
                copy.start()
                to_x.append(copy)

    def summed(m, rows):
        return (half[m, x, rows, :] + xgot[m, 0, rows, :]) + (xgot[m, 1, rows, :] + xgot[m, 2, rows, :])

    here = pl.ds(pl.multiple_of(x * 128, 128), 128)
    for m in range(2):
        for copy in to_x[3 * m : 3 * m + 3]:
            copy.wait_recv()
        if m == 0:
            for k in range(4):
                inverse = 1.0 / summed(0, pl.ds(128 + 8 * k, 8))
                tcol[pl.ds(k * 128, 128), :] = jnp.broadcast_to(inverse[0:1, :], (128, 128)).T
            per_column = summed(0, pl.ds(160, 8)) / summed(0, pl.ds(pl.multiple_of(128 + 8 * x, 8), 8))
            per_column = jnp.broadcast_to(per_column[0:1, :], (32, 128))
            pl.semaphore_wait(sheet_sem, 7)
        for k in range(4):
            tf = 4 * k + 2 * m + c
            rows = pl.ds(pl.multiple_of(tf * 32, 32), 32)
            fin[4 * m + k] = summed(m, pl.ds(k * 32, 32)) * (per_column * tcol[rows, :])
            is_self = jnp.logical_and(tf == f, owner_p == p)

            @pl.when(is_self)
            def _():
                pltpu.make_async_copy(fin.at[4 * m + k], out.at[zh % 2, :, here], fin_recv).start()

            @pl.when(jnp.logical_not(is_self))
            def _():
                pltpu.make_async_remote_copy(
                    src_ref=fin.at[4 * m + k], dst_ref=out.at[zh % 2, :, here], send_sem=fin_send, recv_sem=fin_recv,
                    device_id={"frame": tf, "pix": owner_p}, device_id_type=MESH,
                ).start()

    pltpu.make_async_copy(out, out, fin_recv).wait()
    o_ref[...] = out[...]
    for copy in to_x:
        copy.wait_send()
    sent = packed.at[pl.ds(0, 63)]
    pltpu.make_async_copy(sent, sent, send_sem).wait()

    @pl.when(to_self)
    def _():
        some = fin.at[pl.ds(0, 7)]
        pltpu.make_async_copy(some, some, fin_send).wait()

    @pl.when(jnp.logical_not(to_self))
    def _():
        pltpu.make_async_copy(fin, fin, fin_send).wait()


def body(intensity, labels):
    dma = pltpu.SemaphoreType.DMA
    return pl.pallas_call(
        kernel,
        out_shape=jax.ShapeDtypeStruct((2, 32, 512), F32),
        in_specs=[pl.BlockSpec(memory_space=pl.ANY)] * 2,
        out_specs=pl.BlockSpec(memory_space=pltpu.VMEM),
        scratch_shapes=[
            pltpu.VMEM((64, 128), I32),
            pltpu.VMEM((32, 8192), BF16),
            pltpu.VMEM((4096, 128), BF16),
            pltpu.VMEM((128, 8192), BF16),
            pltpu.VMEM((128, 8192), BF16),
            pltpu.VMEM((4096, 256), F32),
            pltpu.VMEM((128, 128), I32),
            pltpu.VMEM((1024, 128), I32),
            pltpu.VMEM((64, 32, 128), BF16),
            pltpu.VMEM((4, 512, 128), BF16),
            pltpu.VMEM((40, 128), F32),
            pltpu.VMEM((40, 128), F32),
            pltpu.VMEM((2, 4, 128, 128), F32),
            pltpu.VMEM((2, 4, 128, 128), F32),
            pltpu.VMEM((2, 4, MSG, 128), F32),
            pltpu.VMEM((2, 3, MSG, 128), F32),
            pltpu.VMEM((512, 128), F32),
            pltpu.VMEM((8, 32, 128), F32),
            pltpu.VMEM((2, 32, 512), F32),
            dma((2,)), pltpu.SemaphoreType.REGULAR, pltpu.SemaphoreType.REGULAR, dma, dma,
            dma((9,)), dma((9,)), dma((2, 3)), dma((2, 3)), dma, dma,
        ],
        compiler_params=pltpu.CompilerParams(
            collective_id=0, has_side_effects=True, vmem_limit_bytes=60 << 20
        ),
        name="two_time",
    )(labels.reshape(64, 128), intensity)


def solution(mesh):
    return jax.shard_map(
        body,
        mesh=mesh,
        in_specs=(P("frame", "pix"), P("pix")),
        out_specs=P("pix", "frame", None),
        check_vma=False,
    )
```

```python
import jax
import jax.numpy as jnp
from jax import lax
from jax.experimental import pallas as pl
from jax.experimental.pallas import tpu as pltpu
from jax.sharding import PartitionSpec as P

MESH = pl.DeviceIdType.MESH
BF16, F32, I32 = jnp.bfloat16, jnp.float32, jnp.int32
I16 = jnp.int16
LEVELS = 12944.0


def code(value):
    return ((jnp.sqrt(value) * LEVELS + 0.5).astype(I32) - 32768).astype(I16)


def decode(coded):
    root = (coded.astype(I32) + 32768).astype(F32) * (1.0 / LEVELS)
    return root * root


def iota(shape, dim):
    return lax.broadcasted_iota(I32, shape, dim)


def slot_sources(lab, onehot, weighted, ranked, cum, idx):
    bins = iota((64, 128), 0)
    lane = iota((64, 128), 1).astype(F32)
    for i in range(64):
        member = (lab[i : i + 1, :] == bins).astype(F32)
        onehot[pl.ds(i * 64, 64), :] = member.astype(BF16)
        weighted[0:64, pl.ds(i * 128, 128)] = (member * (i + 1.0)).astype(BF16)
        weighted[64:128, pl.ds(i * 128, 128)] = (member * lane).astype(BF16)
    row, col = iota((128, 256), 0), iota((128, 256), 1)
    upto = ((row <= col) | (col >= 128)).astype(F32).astype(BF16)
    cum[...] = jnp.dot(onehot[...], upto, preferred_element_type=F32)
    before = jnp.zeros((64, 128), F32)
    slot = iota((128, 128), 0).astype(F32)
    for i in range(64):
        member = onehot[pl.ds(i * 64, 64), :].astype(F32)
        through = cum[pl.ds(i * 64, 64), 0:128] + before
        rank = jnp.sum(member * through, axis=0, keepdims=True) - 1.0
        before = before + cum[pl.ds(i * 64, 64), 128:256]
        ranked[:, pl.ds(i * 128, 128)] = (slot == rank).astype(F32).astype(BF16)
    found = lax.dot_general(
        weighted[...], ranked[...], (((1,), (1,)), ((), ())), preferred_element_type=F32
    )
    idx[...] = found.astype(I32)


def kernel(
    lab_hbm, x_hbm, o_ref,
    lab, xin, onehot, weighted, ranked, cum, idx, src, packed, met, tot, part, got, own, per_column, tcol, kept, xsent, xgot, fin, out,
    load_sem, line_sem, sheet_sem, send_sem, met_sem, tot_send, tot_recv, core_send, core_recv, x_send, x_recv, fin_send, fin_recv,
):
    f, p = lax.axis_index("frame"), lax.axis_index("pix")
    zh, y = f // 4, f % 4
    zl, x, c = p // 8, (p // 2) % 4, p % 2
    z = zh * 4 + zl
    own_bin = zl * 16 + y * 4 + zh
    owner_p = zl * 8 + y * 2 + zh // 2
    to_self = jnp.logical_and(owner_p == p, y % 2 == c)

    load_lab = pltpu.make_async_copy(lab_hbm, lab, load_sem.at[0])
    load_x = pltpu.make_async_copy(x_hbm, xin, load_sem.at[1])
    load_lab.start()
    load_x.start()

    def on_sheet(dy, dz):
        ty, tz = lax.rem(y + dy, 4), lax.rem(z + dz, 16)
        tzl, tzh = lax.rem(tz, 4), lax.div(tz, 4)
        return tzh * 4 + ty, tzl * 8 + x * 2 + c, tzl * 16 + ty * 4 + tzh

    def signal(sem, tf, tp):
        pl.semaphore_signal(sem, inc=1, device_id={"frame": tf, "pix": tp}, device_id_type=MESH)

    def beside(dx, dc):
        return zl * 8 + lax.rem(x + dx, 4) * 2 + (c if dc == 0 else 1 - c)

    others = [(dx, dc) for dx in range(4) for dc in range(2) if (dx, dc) != (0, 0)]
    other_core = beside(0, 1)

    barrier = pltpu.get_barrier_semaphore()
    for d in range(1, 16):
        signal(barrier, *on_sheet(0, d)[:2])
    for d in range(1, 4):
        signal(barrier, *on_sheet(d, 0)[:2])
    for dx, dc in others:
        signal(barrier, f, beside(dx, dc))

    load_lab.wait()
    slot_sources(lab, onehot, weighted, ranked, cum, idx)
    load_x.wait()
    for i in range(64):
        a = (xin[0:16, pl.ds(i * 128, 128)].astype(F32) * 2048.0).astype(I32)
        b = (xin[16:32, pl.ds(i * 128, 128)].astype(F32) * 2048.0).astype(I32)
        src[pl.ds(i * 16, 16), :] = a + b * 65536

    pl.semaphore_wait(barrier, 25)
    for d in range(1, 4):
        signal(line_sem, *on_sheet(d, 0)[:2])

    def pack(r, j):
        tile = jnp.broadcast_to(idx[pl.ds(r, 1), :], (8, 128))
        lane = jnp.broadcast_to(idx[pl.ds(64 + r, 1), :], (8, 128))
        upper = jnp.zeros((8, 128), I32)
        lower = jnp.zeros((8, 128), I32)
        for i in range(64):
            here = tile == i + 1
            up = jnp.take_along_axis(src[pl.ds(i * 16, 8), :], lane, axis=1, mode="promise_in_bounds")
            low = jnp.take_along_axis(src[pl.ds(i * 16 + 8, 8), :], lane, axis=1, mode="promise_in_bounds")
            upper = jnp.where(here, up, upper)
            lower = jnp.where(here, low, lower)
        pair = jnp.concatenate([upper, lower], axis=0)
        packed[j, 0:16, :] = ((pair & 0xFFFF).astype(F32) * (1 / 2048)).astype(BF16)
        packed[j, 16:32, :] = ((pair >> 16).astype(F32) * (1 / 2048)).astype(BF16)

    def send_step(j, carry):
        n = lax.rem(j, 16)
        dz = lax.rem(8 + jnp.where(lax.rem(n, 2) == 1, lax.div(n + 1, 2), 16 - lax.div(n, 2)), 16)
        tf, tp, r = on_sheet(lax.div(j, 16), dz)
        pack(r, j)
        pltpu.make_async_remote_copy(
            src_ref=packed.at[j],
            dst_ref=met.at[zl, pl.ds(pl.multiple_of(f * 32, 32), 32), :],
            send_sem=send_sem,
            recv_sem=met_sem,
            device_id={"frame": tf, "pix": tp},
            device_id_type=MESH,
        ).start()
        return carry

    lax.fori_loop(0, 15, send_step, 0)
    pack(own_bin, 15)
    pltpu.make_async_copy(
        packed.at[15], met.at[zl, pl.ds(pl.multiple_of(f * 32, 32), 32), :], met_sem
    ).start()
    pl.semaphore_wait(line_sem, 3)
    for dx, dc in others:
        signal(sheet_sem, f, beside(dx, dc))
    lax.fori_loop(16, 64, send_step, 0)
    pltpu.make_async_copy(met, met, met_sem).wait()

    right = jnp.concatenate([met[k] for k in range(4)], axis=1)
    valid = (right[0:16, :].astype(F32) > 0.0).astype(F32)
    valid = jnp.broadcast_to(valid[0:1, :], (16, 512))
    contract = (((1,), (1,)), ((), ()))

    def product(part_of, core):
        blocks = [pl.ds(pl.multiple_of((4 * k + 2 * part_of + core) * 32, 32), 32) for k in range(4)]
        left = jnp.concatenate(
            [jnp.concatenate([met[k, b, :] for b in blocks], axis=0) for k in range(4)], axis=1
        )
        return lax.dot_general(left, right, contract, preferred_element_type=F32)

    totals = lax.dot_general(valid.astype(BF16), right, contract, preferred_element_type=F32)[0:8]
    count = jnp.broadcast_to(jnp.sum(valid[0:1], axis=1, keepdims=True), (1, 128))
    rows = [totals[0:1, b * 128 : b * 128 + 128] for b in range(4)]
    tot[0] = jnp.concatenate(rows + [count] * 4, axis=0)
    to_all = []
    for k, (dx, dc) in enumerate(others):
        to_all.append(
            pltpu.make_async_remote_copy(
                src_ref=tot.at[0], dst_ref=tot.at[k + 1], send_sem=tot_send, recv_sem=tot_recv,
                device_id={"frame": f, "pix": beside(dx, dc)}, device_id_type=MESH,
            )
        )
        to_all[-1].start()

    def core_copy(source, target, k):
        return pltpu.make_async_remote_copy(
            src_ref=source, dst_ref=target, send_sem=core_send.at[k], recv_sem=core_recv.at[k],
            device_id={"frame": f, "pix": other_core}, device_id_type=MESH,
        )

    order = [(d, lax.rem(x + d, 4)) for d in (2, 1, 3, 0)]
    to_core = []
    for m in range(2):
        theirs = product(m, 1 - c)
        for b in range(4):
            part[m, b] = theirs[:, b * 128 : b * 128 + 128]
        for d, b in order:
            to_core.append(core_copy(part.at[m, b], got.at[m, b], 4 * m + d))
            to_core[-1].start()
    for m in range(2):
        mine = product(m, c)
        for b in range(4):
            own[m, b] = mine[:, b * 128 : b * 128 + 128]

    theirs = tot.at[pl.ds(1, 7)]
    pltpu.make_async_copy(theirs, theirs, tot_recv).wait()
    both = tot[0]
    for k in range(1, 8):
        both = both + tot[k]
    inverse = 1.0 / both
    per_column[...] = inverse * both[4:5, :]
    for k in range(4):
        tcol[k] = jnp.broadcast_to(inverse[k : k + 1, :], (128, 128)).T

    to_x = []
    for m in range(2):
        rows = pl.ds(pl.multiple_of((2 * m + c) * 32, 32), 32)
        per_row = jnp.concatenate([tcol[k, rows, :] for k in range(4)], axis=0)
        for (d, b), copy in zip(order, to_core[4 * m : 4 * m + 4]):
            copy.wait()
            value = (own[m, b] + got[m, b]) * (per_row * per_column[pl.ds(b, 1), :])
            if d == 0:
                kept[m] = value
            else:
                xsent[m, d - 1] = code(value)
                copy = pltpu.make_async_remote_copy(
                    src_ref=xsent.at[m, d - 1], dst_ref=xgot.at[m, d - 1],
                    send_sem=x_send.at[m, d - 1], recv_sem=x_recv.at[m, d - 1],
                    device_id={"frame": f, "pix": beside(d, 0)}, device_id_type=MESH,
                )
                copy.start()
                to_x.append(copy)

    pl.semaphore_wait(sheet_sem, 7)
    here = pl.ds(pl.multiple_of(x * 128, 128), 128)
    for m in range(2):
        for copy in to_x[3 * m : 3 * m + 3]:
            copy.wait_recv()
        whole = (kept[m] + decode(xgot[m, 0])) + (decode(xgot[m, 1]) + decode(xgot[m, 2]))
        for k in range(4):
            tf = 4 * k + 2 * m + c
            fin[4 * m + k] = code(whole[k * 32 : k * 32 + 32, :])
            is_self = jnp.logical_and(tf == f, owner_p == p)

            @pl.when(is_self)
            def _():
                pltpu.make_async_copy(fin.at[4 * m + k], out.at[zh % 2, :, here], fin_recv).start()

            @pl.when(jnp.logical_not(is_self))
            def _():
                pltpu.make_async_remote_copy(
                    src_ref=fin.at[4 * m + k], dst_ref=out.at[zh % 2, :, here], send_sem=fin_send, recv_sem=fin_recv,
                    device_id={"frame": tf, "pix": owner_p}, device_id_type=MESH,
                ).start()

    pltpu.make_async_copy(out, out, fin_recv).wait()
    o_ref[...] = decode(out[...])
    for copy in to_x:
        copy.wait_send()
    pltpu.make_async_copy(theirs, theirs, tot_send).wait()
    sent = packed.at[pl.ds(0, 63)]
    pltpu.make_async_copy(sent, sent, send_sem).wait()

    @pl.when(to_self)
    def _():
        some = fin.at[pl.ds(0, 7)]
        pltpu.make_async_copy(some, some, fin_send).wait()

    @pl.when(jnp.logical_not(to_self))
    def _():
        pltpu.make_async_copy(fin, fin, fin_send).wait()


def body(intensity, labels):
    dma = pltpu.SemaphoreType.DMA
    return pl.pallas_call(
        kernel,
        out_shape=jax.ShapeDtypeStruct((2, 32, 512), F32),
        in_specs=[pl.BlockSpec(memory_space=pl.ANY)] * 2,
        out_specs=pl.BlockSpec(memory_space=pltpu.VMEM),
        scratch_shapes=[
            pltpu.VMEM((64, 128), I32),
            pltpu.VMEM((32, 8192), BF16),
            pltpu.VMEM((4096, 128), BF16),
            pltpu.VMEM((128, 8192), BF16),
            pltpu.VMEM((128, 8192), BF16),
            pltpu.VMEM((4096, 256), F32),
            pltpu.VMEM((128, 128), I32),
            pltpu.VMEM((1024, 128), I32),
            pltpu.VMEM((64, 32, 128), BF16),
            pltpu.VMEM((4, 512, 128), BF16),
            pltpu.VMEM((8, 8, 128), F32),
            pltpu.VMEM((2, 4, 128, 128), F32),
            pltpu.VMEM((2, 4, 128, 128), F32),
            pltpu.VMEM((2, 4, 128, 128), F32),
            pltpu.VMEM((8, 128), F32),
            pltpu.VMEM((4, 128, 128), F32),
            pltpu.VMEM((2, 128, 128), F32),
            pltpu.VMEM((2, 3, 128, 128), I16),
            pltpu.VMEM((2, 3, 128, 128), I16),
            pltpu.VMEM((8, 32, 128), I16),
            pltpu.VMEM((2, 32, 512), I16),
            dma((2,)), pltpu.SemaphoreType.REGULAR, pltpu.SemaphoreType.REGULAR, dma, dma, dma, dma,
            dma((8,)), dma((8,)), dma((2, 3)), dma((2, 3)), dma, dma,
        ],
        compiler_params=pltpu.CompilerParams(
            collective_id=0, has_side_effects=True, vmem_limit_bytes=60 << 20
        ),
        name="two_time",
    )(labels.reshape(64, 128), intensity)


def solution(mesh):
    return jax.shard_map(
        body,
        mesh=mesh,
        in_specs=(P("frame", "pix"), P("pix")),
        out_specs=P("pix", "frame", None),
        check_vma=False,
    )
```

```python
import math

import jax
import jax.numpy as jnp
from jax import lax
from jax.experimental import pallas as pl
from jax.experimental.pallas import tpu as pltpu
from jax.sharding import PartitionSpec as P

MESH = pl.DeviceIdType.MESH
BF16, F32, I32 = jnp.bfloat16, jnp.float32, jnp.int32
I16 = jnp.int16
LOW_SUM, HIGH_SUM = 5.0, 102500.0
LOW_OUT, HIGH_OUT = 0.0099, 25.7


def code(value, low, high):
    levels = 65534.0 / math.log2(high / low)
    return ((jnp.log2(value) * levels + (0.5 - math.log2(low) * levels)).astype(I32) - 32768).astype(I16)


def decode(coded, low, high):
    step = math.log2(high / low) / 65534.0
    return jnp.exp2((coded.astype(I32) + 32768).astype(F32) * step + math.log2(low))


def iota(shape, dim):
    return lax.broadcasted_iota(I32, shape, dim)


def slot_sources(lab, onehot, weighted, ranked, cum, idx):
    bins = iota((64, 128), 0)
    lane = iota((64, 128), 1).astype(F32)
    for i in range(64):
        member = (lab[i : i + 1, :] == bins).astype(F32)
        onehot[pl.ds(i * 64, 64), :] = member.astype(BF16)
        weighted[0:64, pl.ds(i * 128, 128)] = (member * (i + 1.0)).astype(BF16)
        weighted[64:128, pl.ds(i * 128, 128)] = (member * lane).astype(BF16)
    row, col = iota((128, 256), 0), iota((128, 256), 1)
    upto = ((row <= col) | (col >= 128)).astype(F32).astype(BF16)
    cum[...] = jnp.dot(onehot[...], upto, preferred_element_type=F32)
    before = jnp.zeros((64, 128), F32)
    slot = iota((128, 128), 0).astype(F32)
    for i in range(64):
        member = onehot[pl.ds(i * 64, 64), :].astype(F32)
        through = cum[pl.ds(i * 64, 64), 0:128] + before
        rank = jnp.sum(member * through, axis=0, keepdims=True) - 1.0
        before = before + cum[pl.ds(i * 64, 64), 128:256]
        ranked[:, pl.ds(i * 128, 128)] = (slot == rank).astype(F32).astype(BF16)
    found = lax.dot_general(
        weighted[...], ranked[...], (((1,), (1,)), ((), ())), preferred_element_type=F32
    )
    idx[...] = found.astype(I32)


def kernel(
    lab_hbm, x_hbm, o_ref,
    lab, xin, onehot, weighted, ranked, cum, idx, src, packed, met, tot, part, got, own, inverse, tcol, kept, xsent, xgot, fin, out,
    load_sem, line_sem, sheet_sem, send_sem, met_sem, tot_send, tot_recv, core_send, core_recv, x_send, x_recv, fin_send, fin_recv,
):
    f, p = lax.axis_index("frame"), lax.axis_index("pix")
    zh, y = f // 4, f % 4
    zl, x, c = p // 8, (p // 2) % 4, p % 2
    z = zh * 4 + zl
    own_bin = (zl + 2) % 4 * 16 + y * 4 + zh
    owner_p = own_bin // 2

    load_lab = pltpu.make_async_copy(lab_hbm, lab, load_sem.at[0])
    load_x = pltpu.make_async_copy(x_hbm, xin, load_sem.at[1])
    load_lab.start()
    load_x.start()

    def on_sheet(dy, dz):
        ty, tz = lax.rem(y + dy, 4), lax.rem(z + dz, 16)
        tzl, tzh = lax.rem(tz, 4), lax.div(tz, 4)
        return tzh * 4 + ty, tzl * 8 + x * 2 + c, lax.rem(tzl + 2, 4) * 16 + ty * 4 + tzh

    def signal(sem, tf, tp):
        pl.semaphore_signal(sem, inc=1, device_id={"frame": tf, "pix": tp}, device_id_type=MESH)

    def beside(dx, dc):
        return zl * 8 + lax.rem(x + dx, 4) * 2 + (c if dc == 0 else 1 - c)

    others = [(dx, dc) for dx in range(4) for dc in range(2) if (dx, dc) != (0, 0)]
    other_core = beside(0, 1)

    barrier = pltpu.get_barrier_semaphore()
    for d in range(1, 16):
        signal(barrier, *on_sheet(0, d)[:2])
    for d in range(1, 4):
        signal(barrier, *on_sheet(d, 0)[:2])
    for dx, dc in others:
        signal(barrier, f, beside(dx, dc))

    load_lab.wait()
    slot_sources(lab, onehot, weighted, ranked, cum, idx)
    load_x.wait()
    for i in range(64):
        a = (xin[0:16, pl.ds(i * 128, 128)].astype(F32) * 2048.0).astype(I32)
        b = (xin[16:32, pl.ds(i * 128, 128)].astype(F32) * 2048.0).astype(I32)
        src[pl.ds(i * 16, 16), :] = a + b * 65536

    pl.semaphore_wait(barrier, 25)
    for d in range(1, 4):
        signal(line_sem, *on_sheet(d, 0)[:2])

    def pack(r, j):
        tile = jnp.broadcast_to(idx[pl.ds(r, 1), :], (8, 128))
        lane = jnp.broadcast_to(idx[pl.ds(64 + r, 1), :], (8, 128))
        upper = jnp.zeros((8, 128), I32)
        lower = jnp.zeros((8, 128), I32)
        for i in range(64):
            here = tile == i + 1
            up = jnp.take_along_axis(src[pl.ds(i * 16, 8), :], lane, axis=1, mode="promise_in_bounds")
            low = jnp.take_along_axis(src[pl.ds(i * 16 + 8, 8), :], lane, axis=1, mode="promise_in_bounds")
            upper = jnp.where(here, up, upper)
            lower = jnp.where(here, low, lower)
        pair = jnp.concatenate([upper, lower], axis=0)
        packed[j, 0:16, :] = ((pair & 0xFFFF).astype(F32) * (1 / 2048)).astype(BF16)
        packed[j, 16:32, :] = ((pair >> 16).astype(F32) * (1 / 2048)).astype(BF16)

    def send_step(j, carry):
        n = lax.rem(j, 16)
        dz = lax.rem(8 + jnp.where(lax.rem(n, 2) == 1, lax.div(n + 1, 2), 16 - lax.div(n, 2)), 16)
        tf, tp, r = on_sheet(lax.div(j, 16), dz)
        pack(r, j)
        pltpu.make_async_remote_copy(
            src_ref=packed.at[j],
            dst_ref=met.at[zl, pl.ds(pl.multiple_of(f * 32, 32), 32), :],
            send_sem=send_sem,
            recv_sem=met_sem,
            device_id={"frame": tf, "pix": tp},
            device_id_type=MESH,
        ).start()
        return carry

    lax.fori_loop(0, 15, send_step, 0)
    pack(own_bin, 15)
    pltpu.make_async_copy(
        packed.at[15], met.at[zl, pl.ds(pl.multiple_of(f * 32, 32), 32), :], met_sem
    ).start()
    pl.semaphore_wait(line_sem, 3)
    for dx, dc in others:
        signal(sheet_sem, f, beside(dx, dc))
    lax.fori_loop(16, 64, send_step, 0)
    pltpu.make_async_copy(met, met, met_sem).wait()

    right = jnp.concatenate([met[k] for k in range(4)], axis=1)
    valid = (right[0:16, :].astype(F32) > 0.0).astype(F32)
    valid = jnp.broadcast_to(valid[0:1, :], (16, 512))
    contract = (((1,), (1,)), ((), ()))

    def frame_block(m, core, rel):
        near = jnp.logical_or(rel == 0, rel == 3)
        dz = jnp.where(rel < 2, 6, 2)
        ty = lax.rem(y + jnp.where(near, 2 - m, 3 - 3 * m), 4)
        return lax.div(lax.rem(z + jnp.where(core == 0, dz, 16 - dz), 16), 4) * 4 + ty

    def product(m, core):
        blocks = [pl.ds(pl.multiple_of(frame_block(m, core, rel) * 32, 32), 32) for rel in range(4)]
        left = jnp.concatenate(
            [jnp.concatenate([met[k, b, :] for b in blocks], axis=0) for k in range(4)], axis=1
        )
        return lax.dot_general(left, right, contract, preferred_element_type=F32)

    totals = lax.dot_general(valid.astype(BF16), right, contract, preferred_element_type=F32)[0:8]
    count = jnp.broadcast_to(jnp.sum(valid[0:1], axis=1, keepdims=True), (1, 128))
    rows = [totals[0:1, b * 128 : b * 128 + 128] for b in range(4)]
    tot[0] = jnp.concatenate(rows + [count] * 4, axis=0)
    to_all = []
    for k, (dx, dc) in enumerate(others):
        to_all.append(
            pltpu.make_async_remote_copy(
                src_ref=tot.at[0], dst_ref=tot.at[k + 1], send_sem=tot_send, recv_sem=tot_recv,
                device_id={"frame": f, "pix": beside(dx, dc)}, device_id_type=MESH,
            )
        )
        to_all[-1].start()

    def core_copy(source, target, k):
        return pltpu.make_async_remote_copy(
            src_ref=source, dst_ref=target, send_sem=core_send.at[k], recv_sem=core_recv.at[k],
            device_id={"frame": f, "pix": other_core}, device_id_type=MESH,
        )

    order = [(d, lax.rem(x + d + 4 - y, 4)) for d in (2, 1, 3, 0)]
    to_core = []
    for m in range(2):
        products = product(m, 1 - c)
        for rel in range(4):
            part[m, rel] = products[rel * 32 : rel * 32 + 32, :]
        for d, rel in order:
            to_core.append(core_copy(part.at[m, rel], got.at[m, rel], 4 * m + d))
            to_core[-1].start()
    to_x = []
    for m in range(2):
        products = product(m, c)
        for rel in range(4):
            own[m, rel] = products[rel * 32 : rel * 32 + 32, :]
        for (d, rel), copy in zip(order, to_core[4 * m : 4 * m + 4]):
            copy.wait()
            value = own[m, rel] + got[m, rel]
            if d == 0:
                kept[m] = value
            else:
                xsent[m, d - 1] = code(value, LOW_SUM, HIGH_SUM)
                copy = pltpu.make_async_remote_copy(
                    src_ref=xsent.at[m, d - 1], dst_ref=xgot.at[m, d - 1],
                    send_sem=x_send.at[m, d - 1], recv_sem=x_recv.at[m, d - 1],
                    device_id={"frame": f, "pix": beside(d, 0)}, device_id_type=MESH,
                )
                copy.start()
                to_x.append(copy)

    theirs = tot.at[pl.ds(1, 7)]
    pltpu.make_async_copy(theirs, theirs, tot_recv).wait()
    both = tot[0]
    for k in range(1, 8):
        both = both + tot[k]
    inverse[...] = 1.0 / both
    per_column = inverse[...] * both[4:5, :]
    per_column = jnp.concatenate([per_column[k : k + 1, :] for k in range(4)], axis=1)
    per_row = []
    targets = [frame_block(m, c, order[3][1]) for m in range(2)]
    for m, tf in enumerate(targets):
        tcol[m] = jnp.broadcast_to(inverse[pl.ds(lax.div(tf, 4), 1), :], (128, 128)).T
        rows = pl.ds(pl.multiple_of(lax.rem(tf, 4) * 32, 32), 32)
        per_row.append(jnp.concatenate([tcol[m, rows, :]] * 4, axis=1))

    pl.semaphore_wait(sheet_sem, 7)
    to_owner = []
    for m, tf in enumerate(targets):
        for copy in to_x[3 * m : 3 * m + 3]:
            copy.wait_recv()
        first, second, third = (decode(xgot[m, k], LOW_SUM, HIGH_SUM) for k in range(3))
        whole = (kept[m] + first) + (second + third)
        fin[m] = code(whole * (per_row[m] * per_column), LOW_OUT, HIGH_OUT)
        copy = pltpu.make_async_remote_copy(
            src_ref=fin.at[m], dst_ref=out.at[zh % 2], send_sem=fin_send.at[m], recv_sem=fin_recv,
            device_id={"frame": tf, "pix": owner_p}, device_id_type=MESH,
        )
        copy.start()
        to_owner.append(copy)

    pltpu.make_async_copy(out, out, fin_recv).wait()
    o_ref[...] = decode(out[...], LOW_OUT, HIGH_OUT)
    for copy in to_owner:
        copy.wait_send()
    for copy in to_x:
        copy.wait_send()
    pltpu.make_async_copy(theirs, theirs, tot_send).wait()
    sent = packed.at[pl.ds(0, 63)]
    pltpu.make_async_copy(sent, sent, send_sem).wait()


def body(intensity, labels):
    dma = pltpu.SemaphoreType.DMA
    return pl.pallas_call(
        kernel,
        out_shape=jax.ShapeDtypeStruct((2, 32, 512), F32),
        in_specs=[pl.BlockSpec(memory_space=pl.ANY)] * 2,
        out_specs=pl.BlockSpec(memory_space=pltpu.VMEM),
        scratch_shapes=[
            pltpu.VMEM((64, 128), I32),
            pltpu.VMEM((32, 8192), BF16),
            pltpu.VMEM((4096, 128), BF16),
            pltpu.VMEM((128, 8192), BF16),
            pltpu.VMEM((128, 8192), BF16),
            pltpu.VMEM((4096, 256), F32),
            pltpu.VMEM((128, 128), I32),
            pltpu.VMEM((1024, 128), I32),
            pltpu.VMEM((64, 32, 128), BF16),
            pltpu.VMEM((4, 512, 128), BF16),
            pltpu.VMEM((8, 8, 128), F32),
            pltpu.VMEM((2, 4, 32, 512), F32),
            pltpu.VMEM((2, 4, 32, 512), F32),
            pltpu.VMEM((2, 4, 32, 512), F32),
            pltpu.VMEM((8, 128), F32),
            pltpu.VMEM((2, 128, 128), F32),
            pltpu.VMEM((2, 32, 512), F32),
            pltpu.VMEM((2, 3, 32, 512), I16),
            pltpu.VMEM((2, 3, 32, 512), I16),
            pltpu.VMEM((2, 32, 512), I16),
            pltpu.VMEM((2, 32, 512), I16),
            dma((2,)), pltpu.SemaphoreType.REGULAR, pltpu.SemaphoreType.REGULAR, dma, dma, dma, dma,
            dma((8,)), dma((8,)), dma((2, 3)), dma((2, 3)), dma((2,)), dma,
        ],
        compiler_params=pltpu.CompilerParams(
            collective_id=0, has_side_effects=True, vmem_limit_bytes=60 << 20
        ),
        name="two_time",
    )(labels.reshape(64, 128), intensity)


def solution(mesh):
    return jax.shard_map(
        body,
        mesh=mesh,
        in_specs=(P("frame", "pix"), P("pix")),
        out_specs=P("pix", "frame", None),
        check_vma=False,
    )
```

```python
import math

import jax
import jax.numpy as jnp
from jax import lax
from jax.experimental import pallas as pl
from jax.experimental.pallas import tpu as pltpu
from jax.sharding import PartitionSpec as P

MESH = pl.DeviceIdType.MESH
BF16, F32, I32 = jnp.bfloat16, jnp.float32, jnp.int32
I16 = jnp.int16
LOW_SUM, HIGH_SUM = 5.0, 102500.0
LOW_OUT, HIGH_OUT = 0.0099, 25.7


def code(value, low, high):
    levels = 65534.0 / math.log2(high / low)
    return ((jnp.log2(value) * levels + (0.5 - math.log2(low) * levels)).astype(I32) - 32768).astype(I16)


def decode(coded, low, high):
    step = math.log2(high / low) / 65534.0
    return jnp.exp2((coded.astype(I32) + 32768).astype(F32) * step + math.log2(low))


def iota(shape, dim):
    return lax.broadcasted_iota(I32, shape, dim)


def slot_sources(lab, onehot, weighted, ranked, cum, idx):
    bins = iota((64, 128), 0)
    lane = iota((64, 128), 1).astype(F32)
    for i in range(64):
        member = (lab[i : i + 1, :] == bins).astype(F32)
        onehot[pl.ds(i * 64, 64), :] = member.astype(BF16)
        weighted[0:64, pl.ds(i * 128, 128)] = (member * (i + 1.0)).astype(BF16)
        weighted[64:128, pl.ds(i * 128, 128)] = (member * lane).astype(BF16)
    row, col = iota((128, 256), 0), iota((128, 256), 1)
    upto = ((row <= col) | (col >= 128)).astype(F32).astype(BF16)
    cum[...] = jnp.dot(onehot[...], upto, preferred_element_type=F32)
    before = jnp.zeros((64, 128), F32)
    slot = iota((128, 128), 0).astype(F32)
    for i in range(64):
        member = onehot[pl.ds(i * 64, 64), :].astype(F32)
        through = cum[pl.ds(i * 64, 64), 0:128] + before
        rank = jnp.sum(member * through, axis=0, keepdims=True) - 1.0
        before = before + cum[pl.ds(i * 64, 64), 128:256]
        ranked[:, pl.ds(i * 128, 128)] = (slot == rank).astype(F32).astype(BF16)
    found = lax.dot_general(
        weighted[...], ranked[...], (((1,), (1,)), ((), ())), preferred_element_type=F32
    )
    idx[...] = found.astype(I32)


def kernel(
    lab_hbm, x_hbm, o_ref,
    lab, xin, onehot, weighted, ranked, cum, idx, src, packed, met, tot, part, got, own, inverse, tcol, kept, xsent, xgot, fin, out,
    load_sem, line_sem, sheet_sem, send_sem, met_sem, tot_send, tot_recv, core_send, core_recv, x_send, x_recv, fin_send, fin_recv,
):
    f, p = lax.axis_index("frame"), lax.axis_index("pix")
    zh, y = f // 4, f % 4
    zl, x, c = p // 8, (p // 2) % 4, p % 2
    z = zh * 4 + zl
    own_bin = (zl + 2) % 4 * 16 + y * 4 + zh
    owner_p = own_bin // 2

    load_lab = pltpu.make_async_copy(lab_hbm, lab, load_sem.at[0])
    load_x = pltpu.make_async_copy(x_hbm, xin, load_sem.at[1])
    load_lab.start()
    load_x.start()

    def on_sheet(dy, dz):
        ty, tz = lax.rem(y + dy, 4), lax.rem(z + dz, 16)
        tzl, tzh = lax.rem(tz, 4), lax.div(tz, 4)
        return tzh * 4 + ty, tzl * 8 + x * 2 + c, lax.rem(tzl + 2, 4) * 16 + ty * 4 + tzh

    def signal(sem, tf, tp):
        pl.semaphore_signal(sem, inc=1, device_id={"frame": tf, "pix": tp}, device_id_type=MESH)

    def beside(dx, dc):
        return zl * 8 + lax.rem(x + dx, 4) * 2 + (c if dc == 0 else 1 - c)

    others = [(dx, dc) for dx in range(4) for dc in range(2) if (dx, dc) != (0, 0)]
    other_core = beside(0, 1)

    barrier = pltpu.get_barrier_semaphore()
    for d in range(1, 16):
        signal(barrier, *on_sheet(0, d)[:2])
    for d in range(1, 4):
        signal(barrier, *on_sheet(d, 0)[:2])
    for dx, dc in others:
        signal(barrier, f, beside(dx, dc))

    load_lab.wait()
    slot_sources(lab, onehot, weighted, ranked, cum, idx)
    load_x.wait()
    for i in range(64):
        a = (xin[0:16, pl.ds(i * 128, 128)].astype(F32) * 2048.0).astype(I32)
        b = (xin[16:32, pl.ds(i * 128, 128)].astype(F32) * 2048.0).astype(I32)
        src[pl.ds(i * 16, 16), :] = a + b * 65536

    pl.semaphore_wait(barrier, 25)
    for d in range(1, 4):
        signal(line_sem, *on_sheet(d, 0)[:2])

    def pack(r, j):
        tile = jnp.broadcast_to(idx[pl.ds(r, 1), :], (8, 128))
        lane = jnp.broadcast_to(idx[pl.ds(64 + r, 1), :], (8, 128))
        upper = jnp.zeros((8, 128), I32)
        lower = jnp.zeros((8, 128), I32)
        for i in range(64):
            here = tile == i + 1
            up = jnp.take_along_axis(src[pl.ds(i * 16, 8), :], lane, axis=1, mode="promise_in_bounds")
            low = jnp.take_along_axis(src[pl.ds(i * 16 + 8, 8), :], lane, axis=1, mode="promise_in_bounds")
            upper = jnp.where(here, up, upper)
            lower = jnp.where(here, low, lower)
        pair = jnp.concatenate([upper, lower], axis=0)
        packed[j, 0:16, :] = ((pair & 0xFFFF).astype(F32) * (1 / 2048)).astype(BF16)
        packed[j, 16:32, :] = ((pair >> 16).astype(F32) * (1 / 2048)).astype(BF16)

    def send_step(j, carry):
        n = lax.rem(j, 16)
        dz = lax.rem(8 + jnp.where(lax.rem(n, 2) == 1, lax.div(n + 1, 2), 16 - lax.div(n, 2)), 16)
        tf, tp, r = on_sheet(lax.div(j, 16), dz)
        pack(r, j)
        pltpu.make_async_remote_copy(
            src_ref=packed.at[j],
            dst_ref=met.at[zl, pl.ds(pl.multiple_of(f * 32, 32), 32), :],
            send_sem=send_sem,
            recv_sem=met_sem,
            device_id={"frame": tf, "pix": tp},
            device_id_type=MESH,
        ).start()
        return carry

    lax.fori_loop(0, 15, send_step, 0)
    pack(own_bin, 15)
    pltpu.make_async_copy(
        packed.at[15], met.at[zl, pl.ds(pl.multiple_of(f * 32, 32), 32), :], met_sem
    ).start()
    pl.semaphore_wait(line_sem, 3)
    for dx, dc in others:
        signal(sheet_sem, f, beside(dx, dc))
    lax.fori_loop(16, 64, send_step, 0)
    pltpu.make_async_copy(met, met, met_sem).wait()

    right = jnp.concatenate([met[k] for k in range(4)], axis=1)
    valid = (right[0:16, :].astype(F32) > 0.0).astype(F32)
    valid = jnp.broadcast_to(valid[0:1, :], (16, 512))
    contract = (((1,), (1,)), ((), ()))

    def frame_block(m, core, rel):
        dz = 6 - 4 * m
        ty = lax.rem(y + 6 - rel, 4)
        return lax.div(lax.rem(z + jnp.where(core == 0, dz, 16 - dz), 16), 4) * 4 + ty

    def product(m, core):
        blocks = [pl.ds(pl.multiple_of(frame_block(m, core, rel) * 32, 32), 32) for rel in range(4)]
        left = jnp.concatenate(
            [jnp.concatenate([met[k, b, :] for b in blocks], axis=0) for k in range(4)], axis=1
        )
        return lax.dot_general(left, right, contract, preferred_element_type=F32)

    to_all = []

    def send_totals():
        totals = lax.dot_general(valid.astype(BF16), right, contract, preferred_element_type=F32)[0:8]
        count = jnp.broadcast_to(jnp.sum(valid[0:1], axis=1, keepdims=True), (1, 128))
        rows = [totals[0:1, b * 128 : b * 128 + 128] for b in range(4)]
        tot[0] = jnp.concatenate(rows + [count] * 4, axis=0)
        for k, (dx, dc) in enumerate(others):
            to_all.append(
                pltpu.make_async_remote_copy(
                    src_ref=tot.at[0], dst_ref=tot.at[k + 1], send_sem=tot_send, recv_sem=tot_recv,
                    device_id={"frame": f, "pix": beside(dx, dc)}, device_id_type=MESH,
                )
            )
            to_all[-1].start()

    def core_copy(source, target, k):
        return pltpu.make_async_remote_copy(
            src_ref=source, dst_ref=target, send_sem=core_send.at[k], recv_sem=core_recv.at[k],
            device_id={"frame": f, "pix": other_core}, device_id_type=MESH,
        )

    order = [(d, lax.rem(x + d + 4 - y, 4)) for d in (2, 1, 3, 0)]
    to_core = []
    to_x = []
    for m in range(2):
        products = product(m, 1 - c)
        for rel in range(4):
            part[m, rel] = products[rel * 32 : rel * 32 + 32, :]
        for d, rel in order:
            to_core.append(core_copy(part.at[m, rel], got.at[m, rel], 4 * m + d))
            to_core[-1].start()
        if m == 0:
            send_totals()
        products = product(m, c)
        for rel in range(4):
            own[m, rel] = products[rel * 32 : rel * 32 + 32, :]
        for (d, rel), copy in zip(order, to_core[4 * m : 4 * m + 4]):
            copy.wait()
            value = own[m, rel] + got[m, rel]
            if d == 0:
                kept[m] = value
            else:
                xsent[m, d - 1] = code(value, LOW_SUM, HIGH_SUM)
                copy = pltpu.make_async_remote_copy(
                    src_ref=xsent.at[m, d - 1], dst_ref=xgot.at[m, d - 1],
                    send_sem=x_send.at[m, d - 1], recv_sem=x_recv.at[m, d - 1],
                    device_id={"frame": f, "pix": beside(d, 0)}, device_id_type=MESH,
                )
                copy.start()
                to_x.append(copy)

    theirs = tot.at[pl.ds(1, 7)]
    pltpu.make_async_copy(theirs, theirs, tot_recv).wait()
    both = tot[0]
    for k in range(1, 8):
        both = both + tot[k]
    inverse[...] = 1.0 / both
    per_column = inverse[...] * both[4:5, :]
    per_column = jnp.concatenate([per_column[k : k + 1, :] for k in range(4)], axis=1)
    per_row = []
    targets = [frame_block(m, c, order[3][1]) for m in range(2)]
    for m, tf in enumerate(targets):
        tcol[m] = jnp.broadcast_to(inverse[pl.ds(lax.div(tf, 4), 1), :], (128, 128)).T
        rows = pl.ds(pl.multiple_of(lax.rem(tf, 4) * 32, 32), 32)
        per_row.append(jnp.concatenate([tcol[m, rows, :]] * 4, axis=1))

    pl.semaphore_wait(sheet_sem, 7)
    to_owner = []
    for m, tf in enumerate(targets):
        for copy in to_x[3 * m : 3 * m + 3]:
            copy.wait_recv()
        first, second, third = (decode(xgot[m, k], LOW_SUM, HIGH_SUM) for k in range(3))
        whole = (kept[m] + first) + (second + third)
        fin[m] = code(whole * (per_row[m] * per_column), LOW_OUT, HIGH_OUT)
        copy = pltpu.make_async_remote_copy(
            src_ref=fin.at[m], dst_ref=out.at[zh % 2], send_sem=fin_send.at[m], recv_sem=fin_recv,
            device_id={"frame": tf, "pix": owner_p}, device_id_type=MESH,
        )
        copy.start()
        to_owner.append(copy)

    pltpu.make_async_copy(out, out, fin_recv).wait()
    o_ref[...] = decode(out[...], LOW_OUT, HIGH_OUT)
    for copy in to_owner:
        copy.wait_send()
    for copy in to_x:
        copy.wait_send()
    pltpu.make_async_copy(theirs, theirs, tot_send).wait()
    sent = packed.at[pl.ds(0, 63)]
    pltpu.make_async_copy(sent, sent, send_sem).wait()


def body(intensity, labels):
    dma = pltpu.SemaphoreType.DMA
    return pl.pallas_call(
        kernel,
        out_shape=jax.ShapeDtypeStruct((2, 32, 512), F32),
        in_specs=[pl.BlockSpec(memory_space=pl.ANY)] * 2,
        out_specs=pl.BlockSpec(memory_space=pltpu.VMEM),
        scratch_shapes=[
            pltpu.VMEM((64, 128), I32),
            pltpu.VMEM((32, 8192), BF16),
            pltpu.VMEM((4096, 128), BF16),
            pltpu.VMEM((128, 8192), BF16),
            pltpu.VMEM((128, 8192), BF16),
            pltpu.VMEM((4096, 256), F32),
            pltpu.VMEM((128, 128), I32),
            pltpu.VMEM((1024, 128), I32),
            pltpu.VMEM((64, 32, 128), BF16),
            pltpu.VMEM((4, 512, 128), BF16),
            pltpu.VMEM((8, 8, 128), F32),
            pltpu.VMEM((2, 4, 32, 512), F32),
            pltpu.VMEM((2, 4, 32, 512), F32),
            pltpu.VMEM((2, 4, 32, 512), F32),
            pltpu.VMEM((8, 128), F32),
            pltpu.VMEM((2, 128, 128), F32),
            pltpu.VMEM((2, 32, 512), F32),
            pltpu.VMEM((2, 3, 32, 512), I16),
            pltpu.VMEM((2, 3, 32, 512), I16),
            pltpu.VMEM((2, 32, 512), I16),
            pltpu.VMEM((2, 32, 512), I16),
            dma((2,)), pltpu.SemaphoreType.REGULAR, pltpu.SemaphoreType.REGULAR, dma, dma, dma, dma,
            dma((8,)), dma((8,)), dma((2, 3)), dma((2, 3)), dma((2,)), dma,
        ],
        compiler_params=pltpu.CompilerParams(
            collective_id=0, has_side_effects=True, vmem_limit_bytes=60 << 20
        ),
        name="two_time",
    )(labels.reshape(64, 128), intensity)


def solution(mesh):
    return jax.shard_map(
        body,
        mesh=mesh,
        in_specs=(P("frame", "pix"), P("pix")),
        out_specs=P("pix", "frame", None),
        check_vma=False,
    )
```

```python
import math

import jax
import jax.numpy as jnp
from jax import lax
from jax.experimental import pallas as pl
from jax.experimental.pallas import tpu as pltpu
from jax.sharding import PartitionSpec as P

MESH = pl.DeviceIdType.MESH
BF16, F32, I32 = jnp.bfloat16, jnp.float32, jnp.int32
I16 = jnp.int16
LOW_SUM, HIGH_SUM = 5.0, 102500.0
LOW_OUT, HIGH_OUT = 0.0099, 25.7


def code(value, low, high):
    levels = 65534.0 / math.log2(high / low)
    return ((jnp.log2(value) * levels + (0.5 - math.log2(low) * levels)).astype(I32) - 32768).astype(I16)


def decode(coded, low, high):
    step = math.log2(high / low) / 65534.0
    return jnp.exp2((coded.astype(I32) + 32768).astype(F32) * step + math.log2(low))


def iota(shape, dim):
    return lax.broadcasted_iota(I32, shape, dim)


def slot_sources(lab, onehot, weighted, ranked, cum, idx):
    bins = iota((64, 128), 0)
    lane = iota((64, 128), 1).astype(F32)
    for i in range(64):
        member = (lab[i : i + 1, :] == bins).astype(F32)
        onehot[pl.ds(i * 64, 64), :] = member.astype(BF16)
        weighted[0:64, pl.ds(i * 128, 128)] = (member * (i + 1.0)).astype(BF16)
        weighted[64:128, pl.ds(i * 128, 128)] = (member * lane).astype(BF16)
    row, col = iota((128, 256), 0), iota((128, 256), 1)
    upto = ((row <= col) | (col >= 128)).astype(F32).astype(BF16)
    cum[...] = jnp.dot(onehot[...], upto, preferred_element_type=F32)
    before = jnp.zeros((64, 128), F32)
    slot = iota((128, 128), 0).astype(F32)
    for i in range(64):
        member = onehot[pl.ds(i * 64, 64), :].astype(F32)
        through = cum[pl.ds(i * 64, 64), 0:128] + before
        rank = jnp.sum(member * through, axis=0, keepdims=True) - 1.0
        before = before + cum[pl.ds(i * 64, 64), 128:256]
        ranked[:, pl.ds(i * 128, 128)] = (slot == rank).astype(F32).astype(BF16)
    found = lax.dot_general(
        weighted[...], ranked[...], (((1,), (1,)), ((), ())), preferred_element_type=F32
    )
    idx[...] = found.astype(I32)


def kernel(
    lab_hbm, x_hbm, o_ref,
    lab, xin, onehot, weighted, ranked, cum, idx, src, packed, met, tot, part, got, own, inverse, tcol, kept, xsent, xgot, fin, out,
    load_sem, line_sem, sheet_sem, send_sem, met_sem, tot_send, tot_recv, core_send, core_recv, x_send, x_recv, fin_send, fin_recv,
):
    f, p = lax.axis_index("frame"), lax.axis_index("pix")
    zh, y = f // 4, f % 4
    zl, x, c = p // 8, (p // 2) % 4, p % 2
    z = zh * 4 + zl

    def bin_at(by, bz):
        turned = lax.rem(bz + 2, 16)
        place = jnp.where(turned < 8, turned, 8 + lax.rem(turned + 2, 8))
        return lax.div(place, 4) * 16 + by * 4 + lax.rem(place, 4)

    own_bin = bin_at(y, z)
    owner_p = own_bin // 2

    load_lab = pltpu.make_async_copy(lab_hbm, lab, load_sem.at[0])
    load_x = pltpu.make_async_copy(x_hbm, xin, load_sem.at[1])
    load_lab.start()
    load_x.start()

    def on_sheet(dy, dz):
        ty, tz = lax.rem(y + dy, 4), lax.rem(z + dz, 16)
        tzl, tzh = lax.rem(tz, 4), lax.div(tz, 4)
        return tzh * 4 + ty, tzl * 8 + x * 2 + c, bin_at(ty, tz)

    def signal(sem, tf, tp):
        pl.semaphore_signal(sem, inc=1, device_id={"frame": tf, "pix": tp}, device_id_type=MESH)

    def beside(dx, dc):
        return zl * 8 + lax.rem(x + dx, 4) * 2 + (c if dc == 0 else 1 - c)

    others = [(dx, dc) for dx in range(4) for dc in range(2) if (dx, dc) != (0, 0)]
    other_core = beside(0, 1)

    barrier = pltpu.get_barrier_semaphore()
    for d in range(1, 16):
        signal(barrier, *on_sheet(0, d)[:2])
    for d in range(1, 4):
        signal(barrier, *on_sheet(d, 0)[:2])
    for dx, dc in others:
        signal(barrier, f, beside(dx, dc))

    load_lab.wait()
    slot_sources(lab, onehot, weighted, ranked, cum, idx)
    load_x.wait()
    for i in range(64):
        a = (xin[0:16, pl.ds(i * 128, 128)].astype(F32) * 2048.0).astype(I32)
        b = (xin[16:32, pl.ds(i * 128, 128)].astype(F32) * 2048.0).astype(I32)
        src[pl.ds(i * 16, 16), :] = a + b * 65536

    pl.semaphore_wait(barrier, 25)
    for d in range(1, 4):
        signal(line_sem, *on_sheet(d, 0)[:2])

    def pack(r, j):
        tile = jnp.broadcast_to(idx[pl.ds(r, 1), :], (8, 128))
        lane = jnp.broadcast_to(idx[pl.ds(64 + r, 1), :], (8, 128))
        upper = jnp.zeros((8, 128), I32)
        lower = jnp.zeros((8, 128), I32)
        for i in range(64):
            here = tile == i + 1
            up = jnp.take_along_axis(src[pl.ds(i * 16, 8), :], lane, axis=1, mode="promise_in_bounds")
            low = jnp.take_along_axis(src[pl.ds(i * 16 + 8, 8), :], lane, axis=1, mode="promise_in_bounds")
            upper = jnp.where(here, up, upper)
            lower = jnp.where(here, low, lower)
        pair = jnp.concatenate([upper, lower], axis=0)
        packed[j, 0:16, :] = ((pair & 0xFFFF).astype(F32) * (1 / 2048)).astype(BF16)
        packed[j, 16:32, :] = ((pair >> 16).astype(F32) * (1 / 2048)).astype(BF16)

    def send_step(j, carry):
        across = jnp.logical_and(j >= 8, j < 56)
        n = jnp.where(across, lax.rem(j + 8, 16), jnp.where(j < 8, j, j - 48))
        dy = jnp.where(across, jnp.where(j < 24, 2, jnp.where(j < 40, 1, 3)), 0)
        dz = lax.rem(8 + jnp.where(lax.rem(n, 2) == 1, lax.div(n + 1, 2), 16 - lax.div(n, 2)), 16)
        tf, tp, r = on_sheet(dy, dz)
        pack(r, j)
        pltpu.make_async_remote_copy(
            src_ref=packed.at[j],
            dst_ref=met.at[zl, pl.ds(pl.multiple_of(f * 32, 32), 32), :],
            send_sem=send_sem,
            recv_sem=met_sem,
            device_id={"frame": tf, "pix": tp},
            device_id_type=MESH,
        ).start()
        return carry

    lax.fori_loop(0, 8, send_step, 0)
    pl.semaphore_wait(line_sem, 3)
    for dx, dc in others:
        signal(sheet_sem, f, beside(dx, dc))
    lax.fori_loop(8, 63, send_step, 0)
    pack(own_bin, 63)
    pltpu.make_async_copy(
        packed.at[63], met.at[zl, pl.ds(pl.multiple_of(f * 32, 32), 32), :], met_sem
    ).start()
    pltpu.make_async_copy(met, met, met_sem).wait()

    right = jnp.concatenate([met[k] for k in range(4)], axis=1)
    valid = (right[0:16, :].astype(F32) > 0.0).astype(F32)
    valid = jnp.broadcast_to(valid[0:1, :], (16, 512))
    contract = (((1,), (1,)), ((), ()))

    def frame_block(m, core, rel):
        return (m + 2 * core) * 4 + lax.rem(y + 6 - rel, 4)

    def product(m, core):
        blocks = [pl.ds(pl.multiple_of(frame_block(m, core, rel) * 32, 32), 32) for rel in range(4)]
        left = jnp.concatenate(
            [jnp.concatenate([met[k, b, :] for b in blocks], axis=0) for k in range(4)], axis=1
        )
        return lax.dot_general(left, right, contract, preferred_element_type=F32)

    to_all = []

    def send_totals():
        totals = lax.dot_general(valid.astype(BF16), right, contract, preferred_element_type=F32)[0:8]
        count = jnp.broadcast_to(jnp.sum(valid[0:1], axis=1, keepdims=True), (1, 128))
        rows = [totals[0:1, b * 128 : b * 128 + 128] for b in range(4)]
        tot[0] = jnp.concatenate(rows + [count] * 4, axis=0)
        for k, (dx, dc) in enumerate(others):
            to_all.append(
                pltpu.make_async_remote_copy(
                    src_ref=tot.at[0], dst_ref=tot.at[k + 1], send_sem=tot_send, recv_sem=tot_recv,
                    device_id={"frame": f, "pix": beside(dx, dc)}, device_id_type=MESH,
                )
            )
            to_all[-1].start()

    def core_copy(source, target, k):
        return pltpu.make_async_remote_copy(
            src_ref=source, dst_ref=target, send_sem=core_send.at[k], recv_sem=core_recv.at[k],
            device_id={"frame": f, "pix": other_core}, device_id_type=MESH,
        )

    order = [(d, lax.rem(x + d + 4 - y, 4)) for d in (2, 1, 3, 0)]
    to_core = []
    to_x = []
    for m in range(2):
        products = product(m, 1 - c)
        for rel in range(4):
            part[m, rel] = products[rel * 32 : rel * 32 + 32, :]
        for d, rel in order:
            to_core.append(core_copy(part.at[m, rel], got.at[m, rel], 4 * m + d))
            to_core[-1].start()
        if m == 0:
            send_totals()
        products = product(m, c)
        for rel in range(4):
            own[m, rel] = products[rel * 32 : rel * 32 + 32, :]
        for (d, rel), copy in zip(order, to_core[4 * m : 4 * m + 4]):
            copy.wait()
            value = own[m, rel] + got[m, rel]
            if d == 0:
                kept[m] = value
            else:
                xsent[m, d - 1] = code(value, LOW_SUM, HIGH_SUM)
                copy = pltpu.make_async_remote_copy(
                    src_ref=xsent.at[m, d - 1], dst_ref=xgot.at[m, d - 1],
                    send_sem=x_send.at[m, d - 1], recv_sem=x_recv.at[m, d - 1],
                    device_id={"frame": f, "pix": beside(d, 0)}, device_id_type=MESH,
                )
                copy.start()
                to_x.append(copy)

    theirs = tot.at[pl.ds(1, 7)]
    pltpu.make_async_copy(theirs, theirs, tot_recv).wait()
    both = tot[0]
    for k in range(1, 8):
        both = both + tot[k]
    inverse[...] = 1.0 / both
    per_column = inverse[...] * both[4:5, :]
    per_column = jnp.concatenate([per_column[k : k + 1, :] for k in range(4)], axis=1)
    per_row = []
    targets = [frame_block(m, c, order[3][1]) for m in range(2)]
    for m, tf in enumerate(targets):
        tcol[m] = jnp.broadcast_to(inverse[pl.ds(lax.div(tf, 4), 1), :], (128, 128)).T
        rows = pl.ds(pl.multiple_of(lax.rem(tf, 4) * 32, 32), 32)
        per_row.append(jnp.concatenate([tcol[m, rows, :]] * 4, axis=1))

    pl.semaphore_wait(sheet_sem, 7)
    to_owner = []
    for m, tf in enumerate(targets):
        for copy in to_x[3 * m : 3 * m + 3]:
            copy.wait_recv()
        first, second, third = (decode(xgot[m, k], LOW_SUM, HIGH_SUM) for k in range(3))
        whole = (kept[m] + first) + (second + third)
        fin[m] = code(whole * (per_row[m] * per_column), LOW_OUT, HIGH_OUT)
        copy = pltpu.make_async_remote_copy(
            src_ref=fin.at[m], dst_ref=out.at[own_bin % 2], send_sem=fin_send.at[m], recv_sem=fin_recv,
            device_id={"frame": tf, "pix": owner_p}, device_id_type=MESH,
        )
        copy.start()
        to_owner.append(copy)

    pltpu.make_async_copy(out, out, fin_recv).wait()
    o_ref[...] = decode(out[...], LOW_OUT, HIGH_OUT)
    for copy in to_owner:
        copy.wait_send()
    for copy in to_x:
        copy.wait_send()
    pltpu.make_async_copy(theirs, theirs, tot_send).wait()
    sent = packed.at[pl.ds(0, 63)]
    pltpu.make_async_copy(sent, sent, send_sem).wait()


def body(intensity, labels):
    dma = pltpu.SemaphoreType.DMA
    return pl.pallas_call(
        kernel,
        out_shape=jax.ShapeDtypeStruct((2, 32, 512), F32),
        in_specs=[pl.BlockSpec(memory_space=pl.ANY)] * 2,
        out_specs=pl.BlockSpec(memory_space=pltpu.VMEM),
        scratch_shapes=[
            pltpu.VMEM((64, 128), I32),
            pltpu.VMEM((32, 8192), BF16),
            pltpu.VMEM((4096, 128), BF16),
            pltpu.VMEM((128, 8192), BF16),
            pltpu.VMEM((128, 8192), BF16),
            pltpu.VMEM((4096, 256), F32),
            pltpu.VMEM((128, 128), I32),
            pltpu.VMEM((1024, 128), I32),
            pltpu.VMEM((64, 32, 128), BF16),
            pltpu.VMEM((4, 512, 128), BF16),
            pltpu.VMEM((8, 8, 128), F32),
            pltpu.VMEM((2, 4, 32, 512), F32),
            pltpu.VMEM((2, 4, 32, 512), F32),
            pltpu.VMEM((2, 4, 32, 512), F32),
            pltpu.VMEM((8, 128), F32),
            pltpu.VMEM((2, 128, 128), F32),
            pltpu.VMEM((2, 32, 512), F32),
            pltpu.VMEM((2, 3, 32, 512), I16),
            pltpu.VMEM((2, 3, 32, 512), I16),
            pltpu.VMEM((2, 32, 512), I16),
            pltpu.VMEM((2, 32, 512), I16),
            dma((2,)), pltpu.SemaphoreType.REGULAR, pltpu.SemaphoreType.REGULAR, dma, dma, dma, dma,
            dma((8,)), dma((8,)), dma((2, 3)), dma((2, 3)), dma((2,)), dma,
        ],
        compiler_params=pltpu.CompilerParams(
            collective_id=0, has_side_effects=True, vmem_limit_bytes=60 << 20
        ),
        name="two_time",
    )(labels.reshape(64, 128), intensity)


def solution(mesh):
    return jax.shard_map(
        body,
        mesh=mesh,
        in_specs=(P("frame", "pix"), P("pix")),
        out_specs=P("pix", "frame", None),
        check_vma=False,
    )
```

```python
import math

import jax
import jax.numpy as jnp
from jax import lax
from jax.experimental import pallas as pl
from jax.experimental.pallas import tpu as pltpu
from jax.sharding import PartitionSpec as P

MESH = pl.DeviceIdType.MESH
BF16, F32, I32 = jnp.bfloat16, jnp.float32, jnp.int32
I16 = jnp.int16
LOW_SUM, HIGH_SUM = 5.0, 102500.0
LOW_OUT, HIGH_OUT = 0.0099, 25.7


def code(value, low, high):
    levels = 65534.0 / math.log2(high / low)
    return ((jnp.log2(value) * levels + (0.5 - math.log2(low) * levels)).astype(I32) - 32768).astype(I16)


def decode(coded, low, high):
    step = math.log2(high / low) / 65534.0
    return jnp.exp2((coded.astype(I32) + 32768).astype(F32) * step + math.log2(low))


def iota(shape, dim):
    return lax.broadcasted_iota(I32, shape, dim)


def slot_sources(lab, onehot, weighted, ranked, cum, idx):
    bins = iota((64, 128), 0)
    lane = iota((64, 128), 1).astype(F32)
    for i in range(64):
        member = (lab[i : i + 1, :] == bins).astype(F32)
        onehot[pl.ds(i * 64, 64), :] = member.astype(BF16)
        weighted[0:64, pl.ds(i * 128, 128)] = (member * (i + 1.0)).astype(BF16)
        weighted[64:128, pl.ds(i * 128, 128)] = (member * lane).astype(BF16)
    row, col = iota((128, 256), 0), iota((128, 256), 1)
    upto = ((row <= col) | (col >= 128)).astype(F32).astype(BF16)
    cum[...] = jnp.dot(onehot[...], upto, preferred_element_type=F32)
    before = jnp.zeros((64, 128), F32)
    slot = iota((128, 128), 0).astype(F32)
    for i in range(64):
        member = onehot[pl.ds(i * 64, 64), :].astype(F32)
        through = cum[pl.ds(i * 64, 64), 0:128] + before
        rank = jnp.sum(member * through, axis=0, keepdims=True) - 1.0
        before = before + cum[pl.ds(i * 64, 64), 128:256]
        ranked[:, pl.ds(i * 128, 128)] = (slot == rank).astype(F32).astype(BF16)
    found = lax.dot_general(
        weighted[...], ranked[...], (((1,), (1,)), ((), ())), preferred_element_type=F32
    )
    idx[...] = found.astype(I32)


def kernel(
    lab_hbm, x_hbm, o_ref,
    lab, xin, onehot, weighted, ranked, cum, idx, src, packed, met, tot, part, got, own, inverse, tcol, kept, xsent, xgot, fin, out,
    load_sem, line_sem, sheet_sem, send_sem, met_sem, tot_send, tot_recv, core_send, core_recv, x_send, x_recv, fin_send, fin_recv,
):
    f, p = lax.axis_index("frame"), lax.axis_index("pix")
    zh, y = f // 4, f % 4
    zl, x, c = p // 8, (p // 2) % 4, p % 2
    z = zh * 4 + zl

    def bin_at(by, bz):
        turned = lax.rem(bz + 2, 16)
        place = jnp.where(turned < 8, turned, 8 + lax.rem(turned + 2, 8))
        return lax.div(place, 4) * 16 + by * 4 + lax.rem(place, 4)

    own_bin = bin_at(y, z)
    owner_p = own_bin // 2

    load_lab = pltpu.make_async_copy(lab_hbm, lab, load_sem.at[0])
    load_x = pltpu.make_async_copy(x_hbm, xin, load_sem.at[1])
    load_lab.start()
    load_x.start()

    def on_sheet(dy, dz):
        ty, tz = lax.rem(y + dy, 4), lax.rem(z + dz, 16)
        tzl, tzh = lax.rem(tz, 4), lax.div(tz, 4)
        return tzh * 4 + ty, tzl * 8 + x * 2 + c, bin_at(ty, tz)

    def signal(sem, tf, tp):
        pl.semaphore_signal(sem, inc=1, device_id={"frame": tf, "pix": tp}, device_id_type=MESH)

    def beside(dx, dc):
        return zl * 8 + lax.rem(x + dx, 4) * 2 + (c if dc == 0 else 1 - c)

    others = [(dx, dc) for dx in range(4) for dc in range(2) if (dx, dc) != (0, 0)]
    other_core = beside(0, 1)

    barrier = pltpu.get_barrier_semaphore()
    for d in range(1, 16):
        signal(barrier, *on_sheet(0, d)[:2])
    for d in range(1, 4):
        signal(barrier, *on_sheet(d, 0)[:2])
    for dx, dc in others:
        signal(barrier, f, beside(dx, dc))

    load_lab.wait()
    slot_sources(lab, onehot, weighted, ranked, cum, idx)
    load_x.wait()
    for i in range(64):
        a = (xin[0:16, pl.ds(i * 128, 128)].astype(F32) * 2048.0).astype(I32)
        b = (xin[16:32, pl.ds(i * 128, 128)].astype(F32) * 2048.0).astype(I32)
        src[pl.ds(i * 16, 16), :] = a + b * 65536

    pl.semaphore_wait(barrier, 25)
    for d in range(1, 4):
        signal(line_sem, *on_sheet(d, 0)[:2])

    def pack(r, j):
        tile = jnp.broadcast_to(idx[pl.ds(r, 1), :], (8, 128))
        lane = jnp.broadcast_to(idx[pl.ds(64 + r, 1), :], (8, 128))
        upper = jnp.zeros((8, 128), I32)
        lower = jnp.zeros((8, 128), I32)
        for i in range(64):
            here = tile == i + 1
            up = jnp.take_along_axis(src[pl.ds(i * 16, 8), :], lane, axis=1, mode="promise_in_bounds")
            low = jnp.take_along_axis(src[pl.ds(i * 16 + 8, 8), :], lane, axis=1, mode="promise_in_bounds")
            upper = jnp.where(here, up, upper)
            lower = jnp.where(here, low, lower)
        pair = jnp.concatenate([upper, lower], axis=0)
        packed[j, 0:16, :] = ((pair & 0xFFFF).astype(F32) * (1 / 2048)).astype(BF16)
        packed[j, 16:32, :] = ((pair >> 16).astype(F32) * (1 / 2048)).astype(BF16)

    def send_step(j, carry):
        across = jnp.logical_and(j >= 8, j < 56)
        n = jnp.where(across, lax.rem(j + 8, 16), jnp.where(j < 8, j, j - 48))
        dy = jnp.where(across, jnp.where(j < 24, 2, jnp.where(j < 40, 1, 3)), 0)
        dz = lax.rem(8 + jnp.where(lax.rem(n, 2) == 1, lax.div(n + 1, 2), 16 - lax.div(n, 2)), 16)
        tf, tp, r = on_sheet(dy, dz)
        pack(r, j)
        pltpu.make_async_remote_copy(
            src_ref=packed.at[j],
            dst_ref=met.at[zl, pl.ds(pl.multiple_of(f * 32, 32), 32), :],
            send_sem=send_sem,
            recv_sem=met_sem,
            device_id={"frame": tf, "pix": tp},
            device_id_type=MESH,
        ).start()
        return carry

    lax.fori_loop(0, 8, send_step, 0)
    pl.semaphore_wait(line_sem, 3)
    for dx, dc in others:
        signal(sheet_sem, f, beside(dx, dc))
    lax.fori_loop(8, 63, send_step, 0)
    pack(own_bin, 63)
    pltpu.make_async_copy(
        packed.at[63], met.at[zl, pl.ds(pl.multiple_of(f * 32, 32), 32), :], met_sem
    ).start()
    pltpu.make_async_copy(met, met, met_sem).wait()

    right = jnp.concatenate([met[k] for k in range(4)], axis=1)
    valid = (right[0:16, :].astype(F32) > 0.0).astype(F32)
    valid = jnp.broadcast_to(valid[0:1, :], (16, 512))
    contract = (((1,), (1,)), ((), ()))

    def frame_block(m, core, rel):
        return (m + 2 * core) * 4 + lax.rem(y + 6 - rel, 4)

    def product(m, core):
        blocks = [pl.ds(pl.multiple_of(frame_block(m, core, rel) * 32, 32), 32) for rel in range(4)]
        left = jnp.concatenate(
            [jnp.concatenate([met[k, b, :] for b in blocks], axis=0) for k in range(4)], axis=1
        )
        return lax.dot_general(left, right, contract, preferred_element_type=F32)

    to_all = []

    def send_totals():
        totals = lax.dot_general(valid.astype(BF16), right, contract, preferred_element_type=F32)[0:8]
        count = jnp.broadcast_to(jnp.sum(valid[0:1], axis=1, keepdims=True), (1, 128))
        rows = [totals[0:1, b * 128 : b * 128 + 128] for b in range(4)]
        tot[0] = jnp.concatenate(rows + [count] * 4, axis=0)
        for k, (dx, dc) in enumerate(others):
            to_all.append(
                pltpu.make_async_remote_copy(
                    src_ref=tot.at[0], dst_ref=tot.at[k + 1], send_sem=tot_send, recv_sem=tot_recv,
                    device_id={"frame": f, "pix": beside(dx, dc)}, device_id_type=MESH,
                )
            )
            to_all[-1].start()

    def core_copy(source, target, k):
        return pltpu.make_async_remote_copy(
            src_ref=source, dst_ref=target, send_sem=core_send.at[k], recv_sem=core_recv.at[k],
            device_id={"frame": f, "pix": other_core}, device_id_type=MESH,
        )

    order = [(d, lax.rem(x + d + 4 - y, 4)) for d in (2, 1, 3, 0)]
    to_core = []
    to_x = []
    for m in range(2):
        products = product(m, 1 - c)
        for rel in range(4):
            part[m, rel] = products[rel * 32 : rel * 32 + 32, :]
        for d, rel in order:
            to_core.append(core_copy(part.at[m, rel], got.at[m, rel], 4 * m + d))
            to_core[-1].start()
        if m == 0:
            send_totals()
        products = product(m, c)
        for rel in range(4):
            own[m, rel] = products[rel * 32 : rel * 32 + 32, :]
        for (d, rel), copy in zip(order, to_core[4 * m : 4 * m + 4]):
            copy.wait()
            value = own[m, rel] + got[m, rel]
            if d == 0:
                kept[m] = value
            else:
                xsent[m, d - 1] = code(value, LOW_SUM, HIGH_SUM)
                copy = pltpu.make_async_remote_copy(
                    src_ref=xsent.at[m, d - 1], dst_ref=xgot.at[m, d - 1],
                    send_sem=x_send.at[m, d - 1], recv_sem=x_recv.at[m, d - 1],
                    device_id={"frame": f, "pix": beside(d, 0)}, device_id_type=MESH,
                )
                copy.start()
                to_x.append(copy)

    theirs = tot.at[pl.ds(1, 7)]
    pltpu.make_async_copy(theirs, theirs, tot_recv).wait()
    both = tot[0]
    for k in range(1, 8):
        both = both + tot[k]
    inverse[...] = 1.0 / both
    per_column = inverse[...] * both[4:5, :]
    per_column = jnp.concatenate([per_column[k : k + 1, :] for k in range(4)], axis=1)
    targets = [frame_block(m, c, order[3][1]) for m in range(2)]
    pl.semaphore_wait(sheet_sem, 7)
    to_owner = []
    for m, tf in enumerate(targets):
        tcol[m] = jnp.broadcast_to(inverse[pl.ds(lax.div(tf, 4), 1), :], (128, 128)).T
        rows = pl.ds(pl.multiple_of(lax.rem(tf, 4) * 32, 32), 32)
        per_row = jnp.concatenate([tcol[m, rows, :]] * 4, axis=1)
        for copy in to_x[3 * m : 3 * m + 3]:
            copy.wait_recv()
        first, second, third = (decode(xgot[m, k], LOW_SUM, HIGH_SUM) for k in range(3))
        whole = (kept[m] + first) + (second + third)
        fin[m] = code(whole * (per_row * per_column), LOW_OUT, HIGH_OUT)
        copy = pltpu.make_async_remote_copy(
            src_ref=fin.at[m], dst_ref=out.at[own_bin % 2], send_sem=fin_send.at[m], recv_sem=fin_recv,
            device_id={"frame": tf, "pix": owner_p}, device_id_type=MESH,
        )
        copy.start()
        to_owner.append(copy)

    pltpu.make_async_copy(out, out, fin_recv).wait()
    o_ref[...] = decode(out[...], LOW_OUT, HIGH_OUT)
    for copy in to_owner:
        copy.wait_send()
    for copy in to_x:
        copy.wait_send()
    pltpu.make_async_copy(theirs, theirs, tot_send).wait()
    sent = packed.at[pl.ds(0, 63)]
    pltpu.make_async_copy(sent, sent, send_sem).wait()


def body(intensity, labels):
    dma = pltpu.SemaphoreType.DMA
    return pl.pallas_call(
        kernel,
        out_shape=jax.ShapeDtypeStruct((2, 32, 512), F32),
        in_specs=[pl.BlockSpec(memory_space=pl.ANY)] * 2,
        out_specs=pl.BlockSpec(memory_space=pltpu.VMEM),
        scratch_shapes=[
            pltpu.VMEM((64, 128), I32),
            pltpu.VMEM((32, 8192), BF16),
            pltpu.VMEM((4096, 128), BF16),
            pltpu.VMEM((128, 8192), BF16),
            pltpu.VMEM((128, 8192), BF16),
            pltpu.VMEM((4096, 256), F32),
            pltpu.VMEM((128, 128), I32),
            pltpu.VMEM((1024, 128), I32),
            pltpu.VMEM((64, 32, 128), BF16),
            pltpu.VMEM((4, 512, 128), BF16),
            pltpu.VMEM((8, 8, 128), F32),
            pltpu.VMEM((2, 4, 32, 512), F32),
            pltpu.VMEM((2, 4, 32, 512), F32),
            pltpu.VMEM((2, 4, 32, 512), F32),
            pltpu.VMEM((8, 128), F32),
            pltpu.VMEM((2, 128, 128), F32),
            pltpu.VMEM((2, 32, 512), F32),
            pltpu.VMEM((2, 3, 32, 512), I16),
            pltpu.VMEM((2, 3, 32, 512), I16),
            pltpu.VMEM((2, 32, 512), I16),
            pltpu.VMEM((2, 32, 512), I16),
            dma((2,)), pltpu.SemaphoreType.REGULAR, pltpu.SemaphoreType.REGULAR, dma, dma, dma, dma,
            dma((8,)), dma((8,)), dma((2, 3)), dma((2, 3)), dma((2,)), dma,
        ],
        compiler_params=pltpu.CompilerParams(
            collective_id=0, has_side_effects=True, vmem_limit_bytes=60 << 20
        ),
        name="two_time",
    )(labels.reshape(64, 128), intensity)


def solution(mesh):
    return jax.shard_map(
        body,
        mesh=mesh,
        in_specs=(P("frame", "pix"), P("pix")),
        out_specs=P("pix", "frame", None),
        check_vma=False,
    )
```
